256 devices in a mesh: pipe: 8 (over y, core), tensor: 8 (over x, z_hi), dp: 4 (over z_lo).
Axes of the slice: x: 4, y: 4, z: 8 (z_hi: 2, z_lo: 4; z = z_hi * 4 + z_lo), core: 2. Of those that a mesh axis runs over, the one named last changes fastest.
Arguments:
- encoder_out: bfloat16 [4, 512, 4096], P('dp', 'pipe', 'tensor'), may hold values from -6 to 6
- queries: bfloat16 [8, 4, 512, 4096], P('pipe', 'dp', None, 'tensor'), may hold values from -48 to 48
- ctx_grad: bfloat16 [8, 4, 512, 4096], P('pipe', 'dp', None, 'tensor'), may hold values from -6 to 6
- key_weight: bfloat16 [8, 4096, 4096], P('pipe', 'dp', 'tensor'), may hold values from -0.09375 to 0.09375
- value_weight: bfloat16 [8, 4096, 4096], P('pipe', 'dp', 'tensor'), may hold values from -0.09375 to 0.09375
Outputs:
- query_grad: bfloat16 [8, 4, 512, 4096], P('pipe', 'dp', None, 'tensor')
- key_weight_grad: float32 [8, 4096, 4096], P('pipe', 'dp', 'tensor')
- value_weight_grad: float32 [8, 4096, 4096], P('pipe', 'dp', 'tensor')
- encoder_grad: float32 [4, 512, 4096], P('dp', 'pipe', 'tensor')
The draws below stay inside these ranges and needn't reach their ends.
All inputs are finite; a program needn't handle non-finite values.
Results may differ from the reference program's by a relative error of at most 0.014.
The reference program's roundings to bfloat16 on the way (of `key_rows`, `value_rows`, `attention_low`, `score_low`, `key_grad` and `value_grad`) count: a program that leaves them out, or rounds other values in their place, can miss the bound.
Values may be sent and summed in bfloat16 or wider, within the bound.
A program may use at most 128 MiB of HBM per device.

```python
import math
import jax
import jax.numpy as jnp
from jax import lax

D = 4096
H = 16
DH = 256
SEQ_DEV = 1
S_ENC = 512
S_DEC = 512
HD = 4096
SECTIONS = 8
BATCH = 4
N_DP = 4


def draw_queries(key, part):
    key = jax.random.fold_in(key, 11)
    normal_key = jax.random.fold_in(key, 0)
    values = jax.random.normal(normal_key, (SECTIONS, BATCH, S_DEC, HD), jnp.float32)
    values = jnp.clip(values, -6.0, 6.0)
    return values.astype(jnp.bfloat16)


def shard_levels(rng, dims, cuts, least, largest):
    level = 1.0
    for axis_at, shards_of in cuts:
        draws = jax.random.uniform(jax.random.fold_in(jax.random.fold_in(rng, 6), axis_at), (shards_of,), jnp.float32, least / len(cuts), largest / len(cuts))
        level = level * jnp.repeat(jnp.exp(draws), dims[axis_at] // shards_of).reshape((-1,) + (1,) * (len(dims) - 1 - axis_at))
    return level


def scatter_about(own_key, dims, spread, most, cuts=(), held_as=jnp.bfloat16):
    drawn = spread * jax.random.normal(own_key, dims, jnp.float32)
    if cuts:
        drawn = drawn * shard_levels(own_key, dims, cuts, -0.22, 0.18)
    return jnp.clip(drawn, -most, most).astype(held_as)


def setup_inputs(seed: int = 0) -> dict:
    splits = jax.random.split(jax.random.key(seed), 6)
    return {
        "encoder_out": scatter_about(splits[0], (BATCH, S_ENC, D), 1.0, 6.0, ((0, 4), (1, 8), (2, 8))),
        "queries": draw_queries(jax.random.fold_in(splits[5], 71), 0),
        "ctx_grad": scatter_about(splits[2], (SECTIONS, BATCH, S_DEC, HD), 1.0, 6.0, ((0, 8), (1, 4), (3, 8))),
        "key_weight": scatter_about(splits[3], (SECTIONS, D, HD), D ** -0.5, 0.09375, ((0, 8), (1, 4), (2, 8))),
        "value_weight": scatter_about(splits[4], (SECTIONS, D, HD), D ** -0.5, 0.09375, ((0, 8), (1, 4), (2, 8))),
    }


def reference(encoder_out, queries, ctx_grad, key_weight, value_weight):
    batch_n, enc_len, model_width = encoder_out.shape
    enc_flat = encoder_out.reshape(batch_n * enc_len, model_width)
    scale_q = 1.0 / math.sqrt(DH)
    group_rows = SEQ_DEV * enc_len

    def per_section(packed):
        query_s, ctx_s, wkey_s, wval_s = packed
        key_rows = jnp.dot(enc_flat, wkey_s, preferred_element_type=jnp.float32).astype(jnp.bfloat16)
        value_rows = jnp.dot(enc_flat, wval_s, preferred_element_type=jnp.float32).astype(jnp.bfloat16)
        key_heads = key_rows.reshape(batch_n, enc_len, H, DH).astype(jnp.float32)
        value_heads = value_rows.reshape(batch_n, enc_len, H, DH).astype(jnp.float32)
        query_heads = query_s.reshape(batch_n, S_DEC, H, DH).astype(jnp.float32)
        grad_heads = ctx_s.reshape(batch_n, S_DEC, H, DH).astype(jnp.float32)
        scores = jnp.einsum('bqhd,bkhd->bhqk', query_heads, key_heads) * scale_q
        attention = jax.nn.softmax(scores, axis=-1)
        attention_low = lax.optimization_barrier(attention.astype(jnp.bfloat16)).astype(jnp.float32)
        prob_grad = jnp.einsum('bqhd,bkhd->bhqk', grad_heads, value_heads)
        score_grad = attention * (prob_grad - lax.optimization_barrier(jnp.sum(prob_grad * attention, axis=-1, keepdims=True)))
        score_low = lax.optimization_barrier((score_grad * scale_q).astype(jnp.bfloat16)).astype(jnp.float32)
        query_grad = jnp.einsum('bhqk,bkhd->bqhd', score_low, key_heads).astype(jnp.bfloat16)
        key_grad = jnp.einsum('bhqk,bqhd->bkhd', score_low, query_heads).astype(jnp.bfloat16)
        value_grad = jnp.einsum('bhqk,bqhd->bkhd', attention_low, grad_heads).astype(jnp.bfloat16)
        key_grad = key_grad.reshape(batch_n * enc_len, HD)
        value_grad = value_grad.reshape(batch_n * enc_len, HD)
        enc_term = jnp.dot(key_grad, wkey_s.T, preferred_element_type=jnp.float32)
        enc_term = enc_term + jnp.dot(value_grad, wval_s.T, preferred_element_type=jnp.float32)
        wkey_grad = jnp.zeros((model_width, HD), jnp.float32)
        wval_grad = jnp.zeros((model_width, HD), jnp.float32)
        for group in range(N_DP):
            enc_group = enc_flat[group * group_rows:(group + 1) * group_rows]
            key_part = jnp.dot(enc_group.T, key_grad[group * group_rows:(group + 1) * group_rows], preferred_element_type=jnp.float32).astype(jnp.bfloat16)
            val_part = jnp.dot(enc_group.T, value_grad[group * group_rows:(group + 1) * group_rows], preferred_element_type=jnp.float32).astype(jnp.bfloat16)
            key_part, val_part = lax.optimization_barrier((key_part, val_part))
            wkey_grad = wkey_grad + key_part.astype(jnp.float32)
            wval_grad = wval_grad + val_part.astype(jnp.float32)
        return (query_grad.reshape(batch_n, S_DEC, HD), wkey_grad, wval_grad, enc_term)
    outputs = lax.map(per_section, (queries, ctx_grad, key_weight, value_weight))
    encoder_grad = lax.optimization_barrier(jnp.sum(outputs[3], axis=0)).reshape(batch_n, enc_len, model_width)
    return (outputs[0], outputs[1], outputs[2], encoder_grad)
```

```python
import math

import jax
import jax.numpy as jnp
from jax import lax
from jax.experimental import pallas as pl
from jax.experimental.pallas import tpu as pltpu
from jax.sharding import PartitionSpec as P

DH = 256
BF = jnp.bfloat16
F32 = jnp.float32
MESH = pl.DeviceIdType.MESH
NT = (((1,), (1,)), ((), ()))
TN = (((0,), (0,)), ((), ()))


def mm(a, b):
    return jnp.dot(a, b, preferred_element_type=F32)


def kernel(
    enc, q, ctx, wk, wv,
    qg, gk, gv, eg,
    encg, enct, wbuf, psk, psv, prk, prv, pown, krow, vrow, sl, al, kvg,
    gsend, grecv, dacc, dsend, drecv, r1, ra_a, ra_b, r2a, r2b, rb_a, rb_b, fin, frecv,
    ssem, rsem, lsem,
):
    pi = lax.axis_index("pipe")
    ti = lax.axis_index("tensor")
    d = lax.axis_index("dp")
    y, c = pi // 2, pi % 2
    x, zh = ti // 2, ti % 2
    xh, xl = x // 2, x % 2
    dh, dl = d // 2, d % 2
    oc, oh, ol = 1 - c, 1 - dh, 1 - dl
    scale = 1.0 / math.sqrt(DH)

    def xpeer(k):
        xx = (x + k) % 4
        return (pi, xx * 2 + zh, d)

    def ypeer(k):
        yy = (y + k) % 4
        return (yy * 2 + c, ti, d)

    peer_c = (y * 2 + oc, ti, d)
    peer_l = (pi, ti, dh * 2 + ol)
    peer_h = (pi, ti, oh * 2 + dl)
    tx = dh * 2 + xl
    td = xh * 2 + dl
    peer_t0 = (pi, tx * 2 + zh, td)
    peer_t1 = (pi, tx * 2 + 1 - zh, td)
    home = xh == dh

    used = [0]

    def send(src, dst, dev):
        k = used[0]
        used[0] += 1
        return pltpu.make_async_remote_copy(
            src, dst, ssem.at[k], rsem.at[k], device_id=dev, device_id_type=MESH
        )

    peers = [peer_c, peer_l, peer_h, peer_t1]
    peers += [xpeer(k) for k in (1, 2, 3)] + [ypeer(k) for k in (1, 2, 3)]
    barrier = pltpu.get_barrier_semaphore()
    for dev in peers:
        pl.semaphore_signal(barrier, inc=1, device_id=dev, device_id_type=MESH)

    @pl.when(jnp.logical_not(home))
    def _():
        pl.semaphore_signal(barrier, inc=1, device_id=peer_t0, device_id_type=MESH)

    owns = []
    for h in range(2):
        for kv, w in enumerate((wk, wv)):
            cp = pltpu.make_async_copy(
                w.at[:, pl.ds(h * DH, DH)], wbuf.at[h, kv, dl], lsem.at[h * 2 + kv]
            )
            cp.start()
            owns.append(cp)

    @pl.when(home)
    def _():
        pl.semaphore_wait(barrier, len(peers))

    @pl.when(jnp.logical_not(home))
    def _():
        pl.semaphore_wait(barrier, len(peers) + 1)

    piece = encg.at[dh, xl * 2 + zh, y, c]
    to_t0 = send(enc, piece, peer_t0)
    to_t1 = send(enc, piece, peer_t1)
    to_t1.start()

    @pl.when(home)
    def _():
        encg[dh, xl * 2 + zh, y, c] = enc[...]

    @pl.when(jnp.logical_not(home))
    def _():
        to_t0.start()

    wsend = [
        [send(w.at[:, pl.ds(h * DH, DH)], wbuf.at[h, kv, dl], peer_l) for kv, w in enumerate((wk, wv))]
        for h in range(2)
    ]
    for cp in wsend[0]:
        cp.start()

    to_t1.wait()

    @pl.when(jnp.logical_not(home))
    def _():
        to_t0.wait()

    xa = pl.ds(xl * 2, 2)
    lo, hi = pl.ds(0, 32), pl.ds(32, 32)
    first = []
    for k in (1, 2, 3):
        ref = encg.at[xh, xa, y, c, lo]
        first.append(send(ref, ref, xpeer(k)))
        ref = encg.at[xh, xa, y, c, hi]
        first.append(send(ref, ref, ypeer(k)))
    for cp in first:
        cp.start()
    for cp in first:
        cp.wait()
    second = []
    for k in (1, 2, 3):
        ref = encg.at[:, :, y, c, lo]
        second.append(send(ref, ref, ypeer(k)))
        ref = encg.at[xh, xa, :, c, hi]
        second.append(send(ref, ref, xpeer(k)))
    for cp in second:
        cp.start()
    for cp in wsend[1]:
        cp.start()
    for cp in second:
        cp.wait()
    third = []
    for s in (oh, dh):
        ref = encg.at[s, :, :, c]
        third.append(send(ref, ref, peer_c))
    for cp in third:
        cp.start()

    def enc_rows(s, r):
        blocks = [encg[s, fb, pl.ds(r * 2, 2)].reshape(256, 512) for fb in range(4)]
        return jnp.concatenate(blocks, axis=1)

    def project(s, h, kv, put):
        def step(r, carry):
            w = wbuf[h, kv].reshape(2048, DH)
            put(pl.ds(pl.multiple_of(r * 256, 256), 256), mm(enc_rows(s, r), w))
            return carry

        lax.fori_loop(0, 2, step, 0)

    def put_k(h):
        def put(rows, v):
            psk[h, rows, :] = v

        return put

    def put_v(h):
        def put(rows, v):
            psv[h, rows, :] = v.astype(BF)

        return put

    def put_own(h, kv):
        def put(rows, v):
            pown[h, kv, rows, :] = v

        return put

    part = []
    for h in range(2):
        for kv in range(2):
            owns[h * 2 + kv].wait()
            wsend[h][kv].wait()
            if h == 0 and kv == 0:
                third[0].wait()
            if kv == 0:
                project(oh, h, 0, put_k(h))
                cp = send(psk.at[h], prk.at[h], peer_h)
            else:
                project(oh, h, 1, put_v(h))
                cp = send(psv.at[h], prv.at[h], peer_h)
            cp.start()
            part.append(cp)
        if h == 0:
            third[1].wait()
        for kv in range(2):
            project(dh, h, kv, put_own(h, kv))

    def flip(n, carry):
        s, fb = n // 4, n % 4
        enct[s, fb] = encg[s, fb].reshape(512, 512).T
        return carry

    lax.fori_loop(0, 8, flip, 0)

    grads = []
    for h in range(2):
        part[2 * h].wait()
        part[2 * h + 1].wait()
        krow[h] = (pown[h, 0] + prk[h]).astype(BF)
        vrow[h] = (pown[h, 1] + prv[h].astype(F32)).astype(BF)
        cols = pl.ds(h * DH, DH)

        def attend(r, carry):
            rows = pl.ds(pl.multiple_of(r * 128, 128), 128)
            kk = krow[h]
            s = lax.dot_general(q[rows, cols], kk, NT, preferred_element_type=F32) * scale
            e = jnp.exp(s - jnp.max(s, axis=-1, keepdims=True))
            a = e / jnp.sum(e, axis=-1, keepdims=True)
            p = lax.dot_general(ctx[rows, cols], vrow[h], NT, preferred_element_type=F32)
            g = a * (p - jnp.sum(p * a, axis=-1, keepdims=True))
            low = (g * scale).astype(BF)
            sl[rows, :] = low
            al[rows, :] = a.astype(BF)
            qg[rows, cols] = mm(low, kk).astype(BF)
            return carry

        lax.fori_loop(0, 4, attend, 0)
        kvg[h, dh, :, 0:DH] = lax.dot_general(
            sl[...], q[:, cols], TN, preferred_element_type=F32
        ).astype(BF)
        kvg[h, dh, :, DH : 2 * DH] = lax.dot_general(
            al[...], ctx[:, cols], TN, preferred_element_type=F32
        ).astype(BF)
        cp = send(kvg.at[h, dh], kvg.at[h, dh], peer_h)
        cp.start()
        grads.append(cp)

    def weight_rows(fb):
        qt, half = fb // 2, pl.ds(pl.multiple_of((fb % 2) * 512, 512), 512)
        return jnp.concatenate([wbuf[h, kv, qt, half, :] for h in range(2) for kv in range(2)], axis=1)

    def encoder_term(s):
        def step(fb, carry):
            both = jnp.concatenate([kvg[0, s], kvg[1, s]], axis=1)
            v = lax.dot_general(both, weight_rows(fb), NT, preferred_element_type=F32)
            dacc[s, fb] = v.reshape(4, 2, 64, 512)
            dsend[s, fb] = dacc[s, fb, :, oc].astype(BF)
            return carry

        lax.fori_loop(0, 4, step, 0)

    core = []

    def encoder_start(s):
        encoder_term(s)
        cp = send(dsend.at[s], drecv.at[s], peer_c)
        cp.start()
        core.append(cp)

    encoder_start(dh)

    def weight_term(h, qt, put):
        def step(z, carry):
            fb = qt * 2 + z
            lhs = jnp.concatenate([enct[0, fb], enct[1, fb]], axis=1)
            rhs = jnp.concatenate([kvg[h, 0], kvg[h, 1]], axis=0)
            put(pl.ds(pl.multiple_of(z * 512, 512), 512), mm(lhs, rhs))
            return carry

        lax.fori_loop(0, 2, step, 0)

    gsent = []

    def weight_send(h):
        def put(rows, v):
            gsend[h, rows, :] = v.astype(BF)

        weight_term(h, ol, put)
        cp = send(gsend.at[h], grecv.at[h], peer_l)
        cp.start()
        gsent.append(cp)

    def weight_own(h):
        cols = pl.ds(h * DH, DH)

        def put(rows, v):
            gk[rows, cols] = v[:, :DH]
            gv[rows, cols] = v[:, DH:]

        weight_term(h, dl, put)

    grads[0].wait()
    weight_send(0)
    weight_own(0)
    grads[1].wait()
    weight_send(1)
    encoder_start(oh)
    core[0].wait()

    def fold_core(s):
        def step(n, carry):
            fb, yy = n // 4, n % 4
            r1[s, fb, yy] = (dacc[s, fb, yy, c] + drecv[s, fb, yy].astype(F32)).astype(BF)
            return carry

        lax.fori_loop(0, 16, step, 0)

    fold_core(dh)
    core[1].wait()
    fold_core(oh)

    one = []
    for k in (1, 2, 3):
        xx = (x + k) % 4
        one.append(send(r1.at[xx // 2, pl.ds((xx % 2) * 2, 2), :, lo], ra_a.at[k - 1], xpeer(k)))
        one.append(send(r1.at[:, :, (y + k) % 4, hi], ra_b.at[k - 1], ypeer(k)))
    for cp in one:
        cp.start()
    weight_own(1)
    for cp in one:
        cp.wait()

    def fold_a(n, carry):
        z, yy = n // 4, n % 4
        v = r1[xh, xl * 2 + z, yy, 0:32, :].astype(F32)
        for k in range(3):
            v = v + ra_a[k, z, yy].astype(F32)
        r2a[z, yy] = v.astype(BF)
        return carry

    lax.fori_loop(0, 8, fold_a, 0)

    def fold_b(n, carry):
        s, fb = n // 4, n % 4
        v = r1[s, fb, y, 32:64, :].astype(F32)
        for k in range(3):
            v = v + ra_b[k, s, fb].astype(F32)
        r2b[s, fb] = v.astype(BF)
        return carry

    lax.fori_loop(0, 8, fold_b, 0)

    two = []
    for k in (1, 2, 3):
        xx = (x + k) % 4
        two.append(send(r2a.at[:, (y + k) % 4], rb_a.at[k - 1], ypeer(k)))
        two.append(send(r2b.at[xx // 2, pl.ds((xx % 2) * 2, 2)], rb_b.at[k - 1], xpeer(k)))
    for cp in two:
        cp.start()
    for cp in two:
        cp.wait()
    for z in range(2):
        v = r2a[z, y].astype(F32)
        for k in range(3):
            v = v + rb_a[k, z].astype(F32)
        fin[z, 0:32, :] = v
        v = r2b[xh, xl * 2 + z].astype(F32)
        for k in range(3):
            v = v + rb_b[k, z].astype(F32)
        fin[z, 32:64, :] = v
    last0 = send(fin.at[zh], frecv.at[0], peer_t0)
    last1 = send(fin.at[1 - zh], frecv.at[1], peer_t1)
    last1.start()

    @pl.when(jnp.logical_not(home))
    def _():
        last0.start()

    for h in range(2):
        gsent[h].wait()
        cols = pl.ds(h * DH, DH)

        def add(r, carry):
            rows = pl.ds(pl.multiple_of(r * 128, 128), 128)
            gk[rows, cols] += grecv[h, rows, 0:DH].astype(F32)
            gv[rows, cols] += grecv[h, rows, DH : 2 * DH].astype(F32)
            return carry

        lax.fori_loop(0, 8, add, 0)

    last1.wait()

    @pl.when(jnp.logical_not(home))
    def _():
        last0.wait()
        eg[...] = frecv[0] + frecv[1]

    @pl.when(home)
    def _():
        eg[...] = fin[zh] + frecv[1]


def shards(encoder_out, queries, ctx_grad, key_weight, value_weight):
    vm = pl.BlockSpec(memory_space=pltpu.VMEM)
    hbm = pl.BlockSpec(memory_space=pl.ANY)
    scratch = [
        ((2, 4, 4, 2, 64, 512), BF),
        ((2, 4, 512, 512), BF),
        ((2, 2, 2, 1024, DH), BF),
        ((2, 512, DH), F32),
        ((2, 512, DH), BF),
        ((2, 512, DH), F32),
        ((2, 512, DH), BF),
        ((2, 2, 512, DH), F32),
        ((2, 512, DH), BF),
        ((2, 512, DH), BF),
        ((512, 512), BF),
        ((512, 512), BF),
        ((2, 2, 512, 512), BF),
        ((2, 1024, 512), BF),
        ((2, 1024, 512), BF),
        ((2, 4, 4, 2, 64, 512), F32),
        ((2, 4, 4, 64, 512), BF),
        ((2, 4, 4, 64, 512), BF),
        ((2, 4, 4, 64, 512), BF),
        ((3, 2, 4, 32, 512), BF),
        ((3, 2, 4, 32, 512), BF),
        ((2, 4, 32, 512), BF),
        ((2, 4, 32, 512), BF),
        ((3, 2, 32, 512), BF),
        ((3, 2, 32, 512), BF),
        ((2, 64, 512), F32),
        ((2, 64, 512), F32),
    ]
    qg, gk, gv, eg = pl.pallas_call(
        kernel,
        out_shape=[
            jax.ShapeDtypeStruct((512, 512), BF),
            jax.ShapeDtypeStruct((1024, 512), F32),
            jax.ShapeDtypeStruct((1024, 512), F32),
            jax.ShapeDtypeStruct((64, 512), F32),
        ],
        in_specs=[vm, vm, vm, hbm, hbm],
        out_specs=[vm, vm, vm, vm],
        scratch_shapes=[pltpu.VMEM(*s) for s in scratch]
        + [
            pltpu.SemaphoreType.DMA((48,)),
            pltpu.SemaphoreType.DMA((48,)),
            pltpu.SemaphoreType.DMA((4,)),
        ],
        compiler_params=pltpu.CompilerParams(
            collective_id=0, has_side_effects=True, vmem_limit_bytes=60 * 1024 * 1024
        ),
        cost_estimate=pl.CostEstimate(
            flops=14_200_000_000, bytes_accessed=8_000_000, transcendentals=600_000
        ),
    )(encoder_out[0], queries[0, 0], ctx_grad[0, 0], key_weight[0], value_weight[0])
    return qg[None, None], gk[None], gv[None], eg[None]


def solution(mesh):
    in_specs = (
        P("dp", "pipe", "tensor"),
        P("pipe", "dp", None, "tensor"),
        P("pipe", "dp", None, "tensor"),
        P("pipe", "dp", "tensor"),
        P("pipe", "dp", "tensor"),
    )
    out_specs = (
        P("pipe", "dp", None, "tensor"),
        P("pipe", "dp", "tensor"),
        P("pipe", "dp", "tensor"),
        P("dp", "pipe", "tensor"),
    )
    return jax.shard_map(shards, mesh=mesh, in_specs=in_specs, out_specs=out_specs, check_vma=False)
```

```python
import math

import jax
import jax.numpy as jnp
from jax import lax
from jax.experimental import pallas as pl
from jax.experimental.pallas import tpu as pltpu
from jax.sharding import PartitionSpec as P

DH = 256
BF = jnp.bfloat16
F32 = jnp.float32
MESH = pl.DeviceIdType.MESH
NT = (((1,), (1,)), ((), ()))
TN = (((0,), (0,)), ((), ()))


def mm(a, b):
    return jnp.dot(a, b, preferred_element_type=F32)


def kernel(
    enc, q, ctx, wk, wv,
    qg, gk, gv, eg,
    encg, enc2, enct, wbuf, psk, psv, prk, prv, pown, krow, vrow, att, sl, al, kvg, kvg2,
    dacc, dsend, drecv, r1, ra_a, ra_b, r2a, r2b, rb_a, rb_b, fin, frecv,
    ssem, rsem, lsem,
):
    pi = lax.axis_index("pipe")
    ti = lax.axis_index("tensor")
    d = lax.axis_index("dp")
    y, c = pi // 2, pi % 2
    x, zh = ti // 2, ti % 2
    xh, xl = x // 2, x % 2
    dh, dl = d // 2, d % 2
    oc, oh, ol = 1 - c, 1 - dh, 1 - dl
    scale = 1.0 / math.sqrt(DH)
    mine = xl * 2 + xh
    lo, hi = pl.ds(0, 32), pl.ds(32, 32)

    def at(xx, zz, dd):
        return (pi, xx * 2 + zz, dd)

    def xpeer(k):
        return at((x + k) % 4, zh, d)

    def ypeer(k):
        return (((y + k) % 4) * 2 + c, ti, d)

    def xblock(k):
        xx = (x + k) % 4
        return (xx % 2) * 2 + xx // 2

    peer_c = (y * 2 + oc, ti, d)
    peer_l = at(x, zh, dh * 2 + ol)
    peer_h = at(x, zh, oh * 2 + dl)
    to_plane = [at(zh * 2 + xl, z, xh * 2 + dl) for z in range(2)]
    from_own = at(dh * 2 + xl, xh, dh * 2 + dl)
    from_oth = at(dh * 2 + xl, xh, oh * 2 + dl)
    loop = jnp.logical_and(xh == dh, zh == xh)
    more = dl != xl
    to_more = [at(dh * 2 + zh, z, xh * 2 + xl) for z in range(2)]
    from_more = at(dh * 2 + dl, xl, xh * 2 + ol)

    used = [0]

    def take(n=1):
        used[0] += n
        return used[0] - n

    def send(src, dst, dev, k=None):
        k = take() if k is None else k
        return pltpu.make_async_remote_copy(
            src, dst, ssem.at[k], rsem.at[k], device_id=dev, device_id_type=MESH
        )

    def two_sems(src, dst, dev, ks, kr):
        return pltpu.make_async_remote_copy(
            src, dst, ssem.at[ks], rsem.at[kr], device_id=dev, device_id_type=MESH
        )

    barrier = pltpu.get_barrier_semaphore()

    def greet(dev):
        pl.semaphore_signal(barrier, inc=1, device_id=dev, device_id_type=MESH)

    peers = [peer_c, peer_l, peer_h]
    peers += [xpeer(k) for k in (1, 2, 3)] + [ypeer(k) for k in (1, 2, 3)]
    for dev in peers:
        greet(dev)
    greet(from_oth)
    greet(from_more)

    @pl.when(jnp.logical_not(loop))
    def _():
        greet(from_own)

    for z in range(2):

        @pl.when(jnp.logical_not(jnp.logical_and(loop, zh == z)))
        def _(z=z):
            greet(to_plane[z])

    owns = []
    for h in range(2):
        for kv, w in enumerate((wk, wv)):
            cp = pltpu.make_async_copy(
                w.at[:, pl.ds(h * DH, DH)], wbuf.at[h, kv, dl], lsem.at[h * 2 + kv]
            )
            cp.start()
            owns.append(cp)

    pl.semaphore_wait(
        barrier, len(peers) + jnp.where(loop, 2, 4) + jnp.where(more, 2, 0)
    )

    ks, kr = take(2), take(2)
    piece = encg.at[dh, xl * 2 + zh, y, c]
    out_piece = [two_sems(enc, piece, to_plane[z], ks + z, kr + dh) for z in range(2)]
    for z in range(2):

        @pl.when(jnp.logical_not(jnp.logical_and(loop, zh == z)))
        def _(z=z):
            out_piece[z].start()

    @pl.when(loop)
    def _():
        encg[dh, mine, y, c] = enc[...]

    ks2, kr2 = take(2), take(1)
    extra = enc2.at[dh, zh, y, c]
    out_more = [two_sems(enc, extra, to_more[z], ks2 + z, kr2) for z in range(2)]

    @pl.when(more)
    def _():
        for z in range(2):
            out_more[z].start()

    wsend = [
        [send(w.at[:, pl.ds(h * DH, DH)], wbuf.at[h, kv, dl], peer_l) for kv, w in enumerate((wk, wv))]
        for h in range(2)
    ]
    wsend[0][0].start()

    def piece_in(s):
        return two_sems(enc, encg.at[s, mine, y, c], from_oth, ks, kr + s)

    def gather_one(s):
        cps = []
        for k in (1, 2, 3):
            ref = encg.at[s, mine, y, c, lo]
            cps.append(send(ref, ref, xpeer(k)))
            ref = encg.at[s, mine, y, c, hi]
            cps.append(send(ref, ref, ypeer(k)))
        for cp in cps:
            cp.start()
        return cps

    def gather_two(s):
        cps = []
        for k in (1, 2, 3):
            ref = encg.at[s, :, y, c, lo]
            cps.append(send(ref, ref, ypeer(k)))
            ref = encg.at[s, mine, :, c, hi]
            cps.append(send(ref, ref, xpeer(k)))
        for cp in cps:
            cp.start()
        return cps

    def gather_core(s):
        ref = encg.at[s, :, :, c]
        cp = send(ref, ref, peer_c)
        cp.start()
        return cp

    def wait_all(cps):
        for cp in cps:
            cp.wait()

    piece_in(oh).wait_recv()
    g1o = gather_one(oh)

    @pl.when(jnp.logical_not(loop))
    def _():
        piece_in(dh).wait_recv()

    g1d = gather_one(dh)
    for z in range(2):

        @pl.when(jnp.logical_not(jnp.logical_and(loop, zh == z)))
        def _(z=z):
            out_piece[z].wait_send()

    wait_all(g1o)
    g2o = gather_two(oh)
    wsend[0][1].start()
    wait_all(g1d)
    wait_all(g2o)
    g3o = gather_core(oh)
    g2d = gather_two(dh)
    g3o.wait()

    def enc_rows(s, r):
        blocks = [encg[s, fb, pl.ds(r * 2, 2)].reshape(256, 512) for fb in range(4)]
        return jnp.concatenate(blocks, axis=1)

    def project(s, h, kv, put):
        def step(r, carry):
            w = wbuf[h, kv].reshape(2048, DH)
            put(pl.ds(pl.multiple_of(r * 256, 256), 256), mm(enc_rows(s, r), w))
            return carry

        lax.fori_loop(0, 2, step, 0)

    part = []

    def project_send(h, kv):
        owns[h * 2 + kv].wait()
        wsend[h][kv].wait()

        def put_k(rows, v):
            psk[h, rows, :] = v

        def put_v(rows, v):
            psv[h, rows, :] = v.astype(BF)

        project(oh, h, kv, put_v if kv else put_k)
        cp = send(psv.at[h], prv.at[h], peer_h) if kv else send(psk.at[h], prk.at[h], peer_h)
        cp.start()
        part.append(cp)

    def project_own(h, kv):
        def put(rows, v):
            pown[h, kv, rows, :] = v

        project(dh, h, kv, put)

    project_send(0, 0)
    wsend[1][0].start()
    project_send(0, 1)
    wsend[1][1].start()
    wait_all(g2d)
    g3d = gather_core(dh)

    @pl.when(more)
    def _():
        for z in range(2):
            out_more[z].wait_send()

    two_sems(enc, enc2.at[xh, xl, y, c], from_more, ks2, kr2).wait_recv()
    m1 = []
    for k in (1, 2, 3):
        ref = enc2.at[xh, xl, y, c]
        m1.append(send(ref, ref, xpeer(k)))
    for cp in m1:
        cp.start()
    g3d.wait()
    project_own(0, 0)
    project_own(0, 1)

    def flip(n, carry):
        s, z = n // 2, n % 2
        enct[s, z] = encg[s, dl * 2 + z].reshape(512, 512).T
        return carry

    lax.fori_loop(0, 4, flip, 0)
    project_send(1, 0)
    project_own(1, 0)
    project_send(1, 1)
    project_own(1, 1)
    wait_all(m1)
    m2 = []
    for k in (1, 2, 3):
        ref = enc2.at[:, :, y, c]
        m2.append(send(ref, ref, ypeer(k)))
    for cp in m2:
        cp.start()

    def flip2(n, carry):
        s, z = n // 2, n % 2
        enct[2 + s, z] = enc2[s, z].reshape(512, 512).T
        return carry

    grads = {}
    near = {}

    def grad_send(h, kv):
        ref = kvg.at[h, dh, kv]
        grads[h, kv] = send(ref, ref, peer_h)
        grads[h, kv].start()
        near[h, kv] = send(ref, kvg2.at[h, dh, kv], peer_l)
        near[h, kv].start()

    def attend(h):
        cols = pl.ds(h * DH, DH)
        part[2 * h].wait()
        krow[h] = (pown[h, 0] + prk[h]).astype(BF)

        def soft(r, carry):
            rows = pl.ds(pl.multiple_of(r * 128, 128), 128)
            s = lax.dot_general(q[rows, cols], krow[h], NT, preferred_element_type=F32) * scale
            e = jnp.exp(s - jnp.max(s, axis=-1, keepdims=True))
            a = e / jnp.sum(e, axis=-1, keepdims=True)
            att[rows, :] = a
            al[rows, :] = a.astype(BF)
            return carry

        lax.fori_loop(0, 4, soft, 0)
        kvg[h, dh, 1] = lax.dot_general(
            al[...], ctx[:, cols], TN, preferred_element_type=F32
        ).astype(BF)
        grad_send(h, 1)
        part[2 * h + 1].wait()
        vrow[h] = (pown[h, 1] + prv[h].astype(F32)).astype(BF)

        def back(r, carry):
            rows = pl.ds(pl.multiple_of(r * 128, 128), 128)
            a = att[rows, :]
            p = lax.dot_general(ctx[rows, cols], vrow[h], NT, preferred_element_type=F32)
            g = a * (p - jnp.sum(p * a, axis=-1, keepdims=True))
            low = (g * scale).astype(BF)
            sl[rows, :] = low
            qg[rows, cols] = mm(low, krow[h]).astype(BF)
            return carry

        lax.fori_loop(0, 4, back, 0)
        kvg[h, dh, 0] = lax.dot_general(
            sl[...], q[:, cols], TN, preferred_element_type=F32
        ).astype(BF)
        grad_send(h, 0)

    attend(0)
    wait_all(m2)
    ref = enc2.at[:, :, :, c]
    m3 = send(ref, ref, peer_c)
    m3.start()
    attend(1)

    far = {}

    def forward(h, kv):
        grads[h, kv].wait()
        far[h, kv] = send(kvg.at[h, oh, kv], kvg2.at[h, oh, kv], peer_l)
        far[h, kv].start()

    def weight_rows(fb, terms):
        qt, half = fb // 2, pl.ds(pl.multiple_of((fb % 2) * 512, 512), 512)
        return jnp.concatenate([wbuf[h, kv, qt, half, :] for h, kv in terms], axis=1)

    def encoder_term(s, terms, add, out):
        def step(fb, carry):
            both = jnp.concatenate([kvg[h, s, kv] for h, kv in terms], axis=1)
            v = lax.dot_general(both, weight_rows(fb, terms), NT, preferred_element_type=F32)
            v = v.reshape(4, 2, 64, 512)
            dacc[s, fb] = dacc[s, fb] + v if add else v
            if out:
                dsend[s, fb] = dacc[s, fb, :, oc].astype(BF)
            return carry

        lax.fori_loop(0, 4, step, 0)

    def reduce_core(s):
        cp = send(dsend.at[s], drecv.at[s], peer_c)
        cp.start()
        return cp

    def reduce_one(s, cp):
        cp.wait()

        def fold(n, carry):
            fb, yy = n // 4, n % 4
            r1[s, fb, yy] = (dacc[s, fb, yy, c] + drecv[s, fb, yy].astype(F32)).astype(BF)
            return carry

        lax.fori_loop(0, 16, fold, 0)
        cps = []
        for k in (1, 2, 3):
            cps.append(send(r1.at[s, xblock(k), :, lo], ra_a.at[s, k - 1], xpeer(k)))
            cps.append(send(r1.at[s, :, (y + k) % 4, hi], ra_b.at[s, k - 1], ypeer(k)))
        for cp in cps:
            cp.start()
        return cps

    def reduce_two(s, cps):
        wait_all(cps)

        def fold(n, carry):
            v = r1[s, mine, n, 0:32, :].astype(F32)
            w = r1[s, n, y, 32:64, :].astype(F32)
            for k in range(3):
                v = v + ra_a[s, k, n].astype(F32)
                w = w + ra_b[s, k, n].astype(F32)
            r2a[s, n] = v.astype(BF)
            r2b[s, n] = w.astype(BF)
            return carry

        lax.fori_loop(0, 4, fold, 0)
        cps = []
        for k in (1, 2, 3):
            cps.append(send(r2a.at[s, (y + k) % 4], rb_a.at[s, k - 1], ypeer(k)))
            cps.append(send(r2b.at[s, xblock(k)], rb_b.at[s, k - 1], xpeer(k)))
        for cp in cps:
            cp.start()
        return cps

    def reduce_sum(s, cps):
        wait_all(cps)
        v = r2a[s, y].astype(F32)
        w = r2b[s, mine].astype(F32)
        for k in range(3):
            v = v + rb_a[s, k].astype(F32)
            w = w + rb_b[s, k].astype(F32)
        fin[s, 0:32, :] = v
        fin[s, 32:64, :] = w

    def weight_term(h, first):
        cols = pl.ds(h * DH, DH)

        def step(z, carry):
            rows = pl.ds(pl.multiple_of(z * 512, 512), 512)
            base, buf = (0, kvg) if first else (2, kvg2)
            lhs = jnp.concatenate([enct[base, z], enct[base + 1, z]], axis=1)
            rhs = jnp.concatenate(
                [jnp.concatenate([buf[h, s, 0], buf[h, s, 1]], axis=1) for s in range(2)], axis=0
            )
            v = mm(lhs, rhs)
            if first:
                gk[rows, cols] = v[:, :DH]
                gv[rows, cols] = v[:, DH:]
            else:
                gk[rows, cols] += v[:, :DH]
                gv[rows, cols] += v[:, DH:]
            return carry

        lax.fori_loop(0, 2, step, 0)

    every = [(0, 0), (0, 1), (1, 1), (1, 0)]
    encoder_term(dh, every, False, True)
    rc = reduce_core(dh)
    rs = reduce_one(dh, rc)
    m3.wait()
    lax.fori_loop(0, 4, flip2, 0)
    forward(0, 1)
    forward(0, 0)
    rs = reduce_two(dh, rs)
    weight_term(0, True)
    reduce_sum(dh, rs)
    kf, krf = take(2), take(2)
    slot = frecv.at[zh]
    out_own = two_sems(fin.at[dh], slot, from_own, kf, krf + zh)
    out_oth = two_sems(fin.at[oh], slot, from_oth, kf + 1, krf + zh)

    @pl.when(jnp.logical_not(loop))
    def _():
        out_own.start()

    @pl.when(loop)
    def _():
        frecv[zh] = fin[dh]

    forward(1, 1)
    encoder_term(oh, every[:3], False, False)
    forward(1, 0)
    encoder_term(oh, every[3:], True, True)
    rc = reduce_core(oh)
    weight_term(1, True)
    rs = reduce_one(oh, rc)
    for kv in (1, 0):
        near[0, kv].wait()
        far[0, kv].wait()
    weight_term(0, False)
    rs = reduce_two(oh, rs)
    reduce_sum(oh, rs)
    out_oth.start()
    for kv in (1, 0):
        near[1, kv].wait()
        far[1, kv].wait()
    weight_term(1, False)

    @pl.when(jnp.logical_not(loop))
    def _():
        out_own.wait_send()

    out_oth.wait_send()
    for z in range(2):

        @pl.when(jnp.logical_not(jnp.logical_and(loop, zh == z)))
        def _(z=z):
            two_sems(fin.at[0], frecv.at[z], to_plane[z], kf, krf + z).wait_recv()

    eg[...] = frecv[0] + frecv[1]


def shards(encoder_out, queries, ctx_grad, key_weight, value_weight):
    vm = pl.BlockSpec(memory_space=pltpu.VMEM)
    hbm = pl.BlockSpec(memory_space=pl.ANY)
    scratch = [
        ((2, 4, 4, 2, 64, 512), BF),
        ((2, 2, 4, 2, 64, 512), BF),
        ((4, 2, 512, 512), BF),
        ((2, 2, 2, 1024, DH), BF),
        ((2, 512, DH), F32),
        ((2, 512, DH), BF),
        ((2, 512, DH), F32),
        ((2, 512, DH), BF),
        ((2, 2, 512, DH), F32),
        ((2, 512, DH), BF),
        ((2, 512, DH), BF),
        ((512, 512), F32),
        ((512, 512), BF),
        ((512, 512), BF),
        ((2, 2, 2, 512, DH), BF),
        ((2, 2, 2, 512, DH), BF),
        ((2, 4, 4, 2, 64, 512), F32),
        ((2, 4, 4, 64, 512), BF),
        ((2, 4, 4, 64, 512), BF),
        ((2, 4, 4, 64, 512), BF),
        ((2, 3, 4, 32, 512), BF),
        ((2, 3, 4, 32, 512), BF),
        ((2, 4, 32, 512), BF),
        ((2, 4, 32, 512), BF),
        ((2, 3, 32, 512), BF),
        ((2, 3, 32, 512), BF),
        ((2, 64, 512), F32),
        ((2, 64, 512), F32),
    ]
    qg, gk, gv, eg = pl.pallas_call(
        kernel,
        out_shape=[
            jax.ShapeDtypeStruct((512, 512), BF),
            jax.ShapeDtypeStruct((1024, 512), F32),
            jax.ShapeDtypeStruct((1024, 512), F32),
            jax.ShapeDtypeStruct((64, 512), F32),
        ],
        in_specs=[vm, vm, vm, hbm, hbm],
        out_specs=[vm, vm, vm, vm],
        scratch_shapes=[pltpu.VMEM(*s) for s in scratch]
        + [
            pltpu.SemaphoreType.DMA((96,)),
            pltpu.SemaphoreType.DMA((96,)),
            pltpu.SemaphoreType.DMA((4,)),
        ],
        compiler_params=pltpu.CompilerParams(
            collective_id=0, has_side_effects=True, vmem_limit_bytes=60 * 1024 * 1024
        ),
        cost_estimate=pl.CostEstimate(
            flops=14_200_000_000, bytes_accessed=8_000_000, transcendentals=600_000
        ),
    )(encoder_out[0], queries[0, 0], ctx_grad[0, 0], key_weight[0], value_weight[0])
    return qg[None, None], gk[None], gv[None], eg[None]


def solution(mesh):
    in_specs = (
        P("dp", "pipe", "tensor"),
        P("pipe", "dp", None, "tensor"),
        P("pipe", "dp", None, "tensor"),
        P("pipe", "dp", "tensor"),
        P("pipe", "dp", "tensor"),
    )
    out_specs = (
        P("pipe", "dp", None, "tensor"),
        P("pipe", "dp", "tensor"),
        P("pipe", "dp", "tensor"),
        P("dp", "pipe", "tensor"),
    )
    return jax.shard_map(shards, mesh=mesh, in_specs=in_specs, out_specs=out_specs, check_vma=False)
```

```python
import math

import jax
import jax.numpy as jnp
from jax import lax
from jax.experimental import pallas as pl
from jax.experimental.pallas import tpu as pltpu
from jax.sharding import PartitionSpec as P

DH = 256
BF = jnp.bfloat16
F32 = jnp.float32
MESH = pl.DeviceIdType.MESH
NT = (((1,), (1,)), ((), ()))
TN = (((0,), (0,)), ((), ()))


def mm(a, b):
    return jnp.dot(a, b, preferred_element_type=F32)


def kernel(
    enc, q, ctx, wk, wv,
    qg_out, gk_out, gv_out, eg,
    qg, gkv, encg, enc2, enct, wbuf, psk, psv, prk, prv, pown, krow, vrow, att, sl, al, kvg, kvg2,
    dacc, dsend, drecv, r1, ra_a, ra_b, r2a, r2b, rb_a, rb_b, fin, frecv,
    ssem, rsem, lsem,
):
    pi = lax.axis_index("pipe")
    ti = lax.axis_index("tensor")
    d = lax.axis_index("dp")
    y, c = pi // 2, pi % 2
    x, zh = ti // 2, ti % 2
    xh, xl = x // 2, x % 2
    dh, dl = d // 2, d % 2
    oc, oh, ol = 1 - c, 1 - dh, 1 - dl
    scale = 1.0 / math.sqrt(DH)
    mine = xl * 2 + xh
    lo, hi = pl.ds(0, 32), pl.ds(32, 32)

    def at(xx, zz, dd):
        return (pi, xx * 2 + zz, dd)

    def xpeer(k):
        return at((x + k) % 4, zh, d)

    def ypeer(k):
        return (((y + k) % 4) * 2 + c, ti, d)

    def xblock(k):
        xx = (x + k) % 4
        return (xx % 2) * 2 + xx // 2

    peer_c = (y * 2 + oc, ti, d)
    peer_l = at(x, zh, dh * 2 + ol)
    peer_h = at(x, zh, oh * 2 + dl)
    to_plane = [at(zh * 2 + xl, z, xh * 2 + dl) for z in range(2)]
    from_own = at(dh * 2 + xl, xh, dh * 2 + dl)
    from_oth = at(dh * 2 + xl, xh, oh * 2 + dl)
    loop = jnp.logical_and(xh == dh, zh == xh)
    more = dl != xl
    to_more = [at(dh * 2 + zh, z, xh * 2 + xl) for z in range(2)]
    from_more = at(dh * 2 + dl, xl, xh * 2 + ol)

    used = [0]

    def take(n=1):
        used[0] += n
        return used[0] - n

    def send(src, dst, dev, k=None):
        k = take() if k is None else k
        return pltpu.make_async_remote_copy(
            src, dst, ssem.at[k], rsem.at[k], device_id=dev, device_id_type=MESH
        )

    def two_sems(src, dst, dev, ks, kr):
        return pltpu.make_async_remote_copy(
            src, dst, ssem.at[ks], rsem.at[kr], device_id=dev, device_id_type=MESH
        )

    barrier = pltpu.get_barrier_semaphore()

    def greet(dev):
        pl.semaphore_signal(barrier, inc=1, device_id=dev, device_id_type=MESH)

    peers = [peer_c, peer_l, peer_h]
    peers += [xpeer(k) for k in (1, 2, 3)] + [ypeer(k) for k in (1, 2, 3)]
    for dev in peers:
        greet(dev)
    greet(from_oth)
    greet(from_more)

    @pl.when(jnp.logical_not(loop))
    def _():
        greet(from_own)

    for z in range(2):

        @pl.when(jnp.logical_not(jnp.logical_and(loop, zh == z)))
        def _(z=z):
            greet(to_plane[z])

    owns = []
    for h in range(2):
        for kv, w in enumerate((wk, wv)):
            cp = pltpu.make_async_copy(
                w.at[:, pl.ds(h * DH, DH)], wbuf.at[h, kv, dl], lsem.at[h * 2 + kv]
            )
            cp.start()
            owns.append(cp)

    pl.semaphore_wait(
        barrier, len(peers) + jnp.where(loop, 2, 4) + jnp.where(more, 2, 0)
    )

    ks, kr = take(2), take(2)
    piece = encg.at[dh, xl * 2 + zh, y, c]
    out_piece = [two_sems(enc, piece, to_plane[z], ks + z, kr + dh) for z in range(2)]
    for z in range(2):

        @pl.when(jnp.logical_not(jnp.logical_and(loop, zh == z)))
        def _(z=z):
            out_piece[z].start()

    @pl.when(loop)
    def _():
        encg[dh, mine, y, c] = enc[...]

    ks2, kr2 = take(2), take(1)
    extra = enc2.at[dh, zh, y, c]
    out_more = [two_sems(enc, extra, to_more[z], ks2 + z, kr2) for z in range(2)]

    wsend = [
        [send(w.at[:, pl.ds(h * DH, DH)], wbuf.at[h, kv, dl], peer_l) for kv, w in enumerate((wk, wv))]
        for h in range(2)
    ]
    wsend[0][0].start()

    def piece_in(s):
        return two_sems(enc, encg.at[s, mine, y, c], from_oth, ks, kr + s)

    def gather_one(s):
        cps = []
        for k in (1, 2, 3):
            ref = encg.at[s, mine, y, c, lo]
            cps.append(send(ref, ref, xpeer(k)))
            ref = encg.at[s, mine, y, c, hi]
            cps.append(send(ref, ref, ypeer(k)))
        for cp in cps:
            cp.start()
        return cps

    def gather_two(s):
        cps = []
        for k in (1, 2, 3):
            ref = encg.at[s, :, y, c, lo]
            cps.append(send(ref, ref, ypeer(k)))
            ref = encg.at[s, mine, :, c, hi]
            cps.append(send(ref, ref, xpeer(k)))
        for cp in cps:
            cp.start()
        return cps

    def gather_core(s):
        ref = encg.at[s, :, :, c]
        cp = send(ref, ref, peer_c)
        cp.start()
        return cp

    def wait_all(cps):
        for cp in cps:
            cp.wait()

    piece_in(oh).wait_recv()
    g1o = gather_one(oh)

    @pl.when(jnp.logical_not(loop))
    def _():
        piece_in(dh).wait_recv()

    @pl.when(more)
    def _():
        for z in range(2):
            out_more[z].start()

    g1d = gather_one(dh)
    for z in range(2):

        @pl.when(jnp.logical_not(jnp.logical_and(loop, zh == z)))
        def _(z=z):
            out_piece[z].wait_send()

    wait_all(g1o)
    g2o = gather_two(oh)
    wsend[0][1].start()
    wait_all(g1d)
    wait_all(g2o)
    g3o = gather_core(oh)
    g2d = gather_two(dh)

    def project_rows(s, h, kv, cc):
        blocks = [encg[s, fb, :, cc].reshape(256, 512) for fb in range(4)]
        v = mm(jnp.concatenate(blocks, axis=1), wbuf[h, kv].reshape(2048, DH))
        return v.reshape(4, 64, DH)

    part = {}

    def project_send(h, kv):
        owns[h * 2 + kv].wait()
        wsend[h][kv].wait()

        def step(cc, carry):
            v = project_rows(oh, h, kv, cc)
            if kv:
                psv[h, :, cc] = v.astype(BF)
            else:
                psk[h, :, cc] = v
            return carry

        lax.fori_loop(0, 2, step, 0)
        cp = send(psv.at[h], prv.at[h], peer_h) if kv else send(psk.at[h], prk.at[h], peer_h)
        cp.start()
        part[h, kv] = [cp]

    def project_own(h, kv):
        def step(cc, carry):
            pown[h, kv, :, cc] = project_rows(dh, h, kv, cc)
            return carry

        lax.fori_loop(0, 2, step, 0)

    owns[0].wait()
    wsend[0][0].wait()
    halves = []
    for cc in (c, oc):
        if len(halves) == 1:
            g3o.wait()
        psk[0, :, cc] = project_rows(oh, 0, 0, cc)
        ref = (psk.at[0, :, cc], prk.at[0, :, cc])
        halves.append(send(*ref, peer_h))
        halves[-1].start()
    part[0, 0] = halves
    wsend[1][0].start()
    project_send(0, 1)
    wsend[1][1].start()
    wait_all(g2d)
    g3d = gather_core(dh)

    @pl.when(more)
    def _():
        for z in range(2):
            out_more[z].wait_send()

    two_sems(enc, enc2.at[xh, xl, y, c], from_more, ks2, kr2).wait_recv()
    m1 = []
    for k in (1, 2, 3):
        ref = enc2.at[xh, xl, y, c]
        m1.append(send(ref, ref, xpeer(k)))
    for cp in m1:
        cp.start()
    g3d.wait()
    project_own(0, 0)
    project_own(0, 1)

    def flip(n, carry):
        s, z = n // 2, n % 2
        enct[s, z] = encg[s, dl * 2 + z].reshape(512, 512).T
        return carry

    lax.fori_loop(0, 4, flip, 0)
    project_send(1, 0)
    project_own(1, 0)
    project_send(1, 1)
    project_own(1, 1)
    wait_all(m1)
    m2 = []
    for k in (1, 2, 3):
        ref = enc2.at[:, :, y, c]
        m2.append(send(ref, ref, ypeer(k)))
    for cp in m2:
        cp.start()

    def flip2(n, carry):
        s, z = n // 2, n % 2
        enct[2 + s, z] = enc2[s, z].reshape(512, 512).T
        return carry

    grads = {}
    near = {}

    def grad_send(h, kv):
        ref = kvg.at[h, dh, kv]
        grads[h, kv] = send(ref, ref, peer_h)
        grads[h, kv].start()
        near[h, kv] = send(ref, kvg2.at[h, dh, kv], peer_l)
        near[h, kv].start()

    def attend(h):
        cols = pl.ds(h * DH, DH)
        wait_all(part[h, 0])
        krow[h] = (pown[h, 0] + prk[h]).reshape(512, DH).astype(BF)

        def soft(r, carry):
            rows = pl.ds(pl.multiple_of(r * 128, 128), 128)
            s = lax.dot_general(q[rows, cols], krow[h], NT, preferred_element_type=F32) * scale
            e = jnp.exp(s - jnp.max(s, axis=-1, keepdims=True))
            a = e / jnp.sum(e, axis=-1, keepdims=True)
            att[rows, :] = a
            al[rows, :] = a.astype(BF)
            return carry

        lax.fori_loop(0, 4, soft, 0)
        kvg[h, dh, 1] = lax.dot_general(
            al[...], ctx[:, cols], TN, preferred_element_type=F32
        ).astype(BF)
        grad_send(h, 1)
        wait_all(part[h, 1])
        vrow[h] = (pown[h, 1] + prv[h].astype(F32)).reshape(512, DH).astype(BF)

        def back(r, carry):
            rows = pl.ds(pl.multiple_of(r * 128, 128), 128)
            a = att[rows, :]
            p = lax.dot_general(ctx[rows, cols], vrow[h], NT, preferred_element_type=F32)
            g = a * (p - jnp.sum(p * a, axis=-1, keepdims=True))
            low = (g * scale).astype(BF)
            sl[rows, :] = low
            qg[rows, cols] = mm(low, krow[h]).astype(BF)
            return carry

        lax.fori_loop(0, 4, back, 0)
        kvg[h, dh, 0] = lax.dot_general(
            sl[...], q[:, cols], TN, preferred_element_type=F32
        ).astype(BF)
        grad_send(h, 0)

    attend(0)
    wait_all(m2)
    ref = enc2.at[:, :, :, c]
    m3 = send(ref, ref, peer_c)
    m3.start()
    attend(1)

    far = {}

    def forward(h, kv):
        grads[h, kv].wait()
        far[h, kv] = send(kvg.at[h, oh, kv], kvg2.at[h, oh, kv], peer_l)
        far[h, kv].start()

    def weight_rows(fb, terms):
        qt, half = fb // 2, pl.ds(pl.multiple_of((fb % 2) * 512, 512), 512)
        return jnp.concatenate([wbuf[h, kv, qt, half, :] for h, kv in terms], axis=1)

    def encoder_term(s, terms, add, out):
        def step(fb, carry):
            both = jnp.concatenate([kvg[h, s, kv] for h, kv in terms], axis=1)
            v = lax.dot_general(both, weight_rows(fb, terms), NT, preferred_element_type=F32)
            v = v.reshape(4, 2, 64, 512)
            dacc[s, fb] = dacc[s, fb] + v if add else v
            if out:
                for n in range(2):
                    for half in range(2):
                        rows = pl.ds(half * 32 + n * 16, 16)
                        dsend[s, n, fb, :, half] = dacc[s, fb, :, oc, rows, :].astype(BF)
            return carry

        lax.fori_loop(0, 4, step, 0)

    def reduce_core(s):
        cps = [send(dsend.at[s, n], drecv.at[s, n], peer_c) for n in range(2)]
        for cp in cps:
            cp.start()
        return cps

    def reduce_one(s, n, cp):
        cp.wait()
        for half in range(2):
            rows = pl.ds(half * 32 + n * 16, 16)

            def fold(fb, carry):
                v = dacc[s, fb, :, c, rows, :] + drecv[s, n, fb, :, half].astype(F32)
                r1[s, n, half, fb] = v.astype(BF)
                return carry

            lax.fori_loop(0, 4, fold, 0)
        cps = []
        for k in (1, 2, 3):
            cps.append(send(r1.at[s, n, 0, xblock(k)], ra_a.at[s, n, k - 1], xpeer(k)))
            cps.append(send(r1.at[s, n, 1, :, (y + k) % 4], ra_b.at[s, n, k - 1], ypeer(k)))
        for cp in cps:
            cp.start()
        return cps

    def reduce_two(s, n, cps):
        wait_all(cps)
        v = r1[s, n, 0, mine].astype(F32)
        w = r1[s, n, 1, :, y].astype(F32)
        for k in range(3):
            v = v + ra_a[s, n, k].astype(F32)
            w = w + ra_b[s, n, k].astype(F32)
        r2a[s, n] = v.astype(BF)
        r2b[s, n] = w.astype(BF)
        cps = []
        for k in (1, 2, 3):
            cps.append(send(r2a.at[s, n, (y + k) % 4], rb_a.at[s, n, k - 1], ypeer(k)))
            cps.append(send(r2b.at[s, n, xblock(k)], rb_b.at[s, n, k - 1], xpeer(k)))
        for cp in cps:
            cp.start()
        return cps

    def reduce_sum(s, n, cps):
        wait_all(cps)
        v = r2a[s, n, y].astype(F32)
        w = r2b[s, n, mine].astype(F32)
        for k in range(3):
            v = v + rb_a[s, n, k].astype(F32)
            w = w + rb_b[s, n, k].astype(F32)
        fin[s, n, 0] = v.astype(BF)
        fin[s, n, 1] = w.astype(BF)

    done = [pltpu.make_async_copy(qg, qg_out, lsem.at[8])]
    done[0].start()

    def weight_term(h, first):
        cols = pl.ds(h * DH, DH)

        def step(z, carry):
            rows = pl.ds(pl.multiple_of(z * 512, 512), 512)
            base, buf = (0, kvg) if first else (2, kvg2)
            lhs = jnp.concatenate([enct[base, z], enct[base + 1, z]], axis=1)
            rhs = jnp.concatenate(
                [jnp.concatenate([buf[h, s, 0], buf[h, s, 1]], axis=1) for s in range(2)], axis=0
            )
            v = mm(lhs, rhs)
            if first:
                gkv[h, 0, rows, :] = v[:, :DH]
                gkv[h, 1, rows, :] = v[:, DH:]
            else:
                gkv[h, 0, rows, :] += v[:, :DH]
                gkv[h, 1, rows, :] += v[:, DH:]
            return carry

        lax.fori_loop(0, 2, step, 0)
        if not first:
            for kv, out in enumerate((gk_out, gv_out)):
                done.append(pltpu.make_async_copy(gkv.at[h, kv], out.at[:, cols], lsem.at[4 + 2 * h + kv]))
                done[-1].start()

    every = [(0, 0), (0, 1), (1, 1), (1, 0)]
    encoder_term(dh, every, False, True)
    rc = reduce_core(dh)
    rs = [reduce_one(dh, n, rc[n]) for n in range(2)]
    m3.wait()
    lax.fori_loop(0, 4, flip2, 0)
    forward(0, 1)
    forward(0, 0)
    rs = [reduce_two(dh, n, rs[n]) for n in range(2)]
    weight_term(0, True)
    for n in range(2):
        reduce_sum(dh, n, rs[n])
    kf, krf = take(4), take(4)

    out_own = [two_sems(fin.at[dh, n], frecv.at[zh, n], from_own, kf + n, krf + 2 * n + zh) for n in range(2)]
    out_oth = [two_sems(fin.at[oh, n], frecv.at[zh, n], from_oth, kf + 2 + n, krf + 2 * n + zh) for n in range(2)]

    @pl.when(jnp.logical_not(loop))
    def _():
        for cp in out_own:
            cp.start()

    @pl.when(loop)
    def _():
        frecv[zh] = fin[dh]

    forward(1, 1)
    encoder_term(oh, every[:3], False, False)
    forward(1, 0)
    encoder_term(oh, every[3:], True, True)
    rc = reduce_core(oh)
    rs = [reduce_one(oh, n, rc[n]) for n in range(2)]
    weight_term(1, True)
    rs[0] = reduce_two(oh, 0, rs[0])
    for kv in (1, 0):
        near[0, kv].wait()
        far[0, kv].wait()
    weight_term(0, False)
    rs[1] = reduce_two(oh, 1, rs[1])
    reduce_sum(oh, 0, rs[0])
    out_oth[0].start()
    reduce_sum(oh, 1, rs[1])
    out_oth[1].start()
    for kv in (1, 0):
        near[1, kv].wait()
        far[1, kv].wait()
    weight_term(1, False)

    @pl.when(jnp.logical_not(loop))
    def _():
        for cp in out_own:
            cp.wait_send()

    for cp in out_oth:
        cp.wait_send()
    for z in range(2):

        @pl.when(jnp.logical_not(jnp.logical_and(loop, zh == z)))
        def _(z=z):
            for n in range(2):
                two_sems(fin.at[0, n], frecv.at[z, n], to_plane[z], kf, krf + 2 * n + z).wait_recv()

    for n in range(2):
        for half in range(2):
            v = frecv[0, n, half].astype(F32) + frecv[1, n, half].astype(F32)
            eg[half * 32 + n * 16 : half * 32 + n * 16 + 16, :] = v
    for cp in done:
        cp.wait()


def hand_over(*arrays):
    n, steps = len(arrays), 2

    def kernel(*refs):
        for i in range(n):
            refs[n + i][...] = refs[i][...]

    specs = [pl.BlockSpec((a.shape[0] // steps, a.shape[1]), lambda i: (i, 0)) for a in arrays]
    return pl.pallas_call(
        kernel,
        grid=(steps,),
        out_shape=[jax.ShapeDtypeStruct(a.shape, a.dtype) for a in arrays],
        in_specs=specs,
        out_specs=specs,
    )(*arrays)


def shards(encoder_out, queries, ctx_grad, key_weight, value_weight):
    vm = pl.BlockSpec(memory_space=pltpu.VMEM)
    hbm = pl.BlockSpec(memory_space=pl.ANY)
    scratch = [
        ((512, 512), BF),
        ((2, 2, 1024, DH), F32),
        ((2, 4, 4, 2, 64, 512), BF),
        ((2, 2, 4, 2, 64, 512), BF),
        ((4, 2, 512, 512), BF),
        ((2, 2, 2, 1024, DH), BF),
        ((2, 4, 2, 64, DH), F32),
        ((2, 4, 2, 64, DH), BF),
        ((2, 4, 2, 64, DH), F32),
        ((2, 4, 2, 64, DH), BF),
        ((2, 2, 4, 2, 64, DH), F32),
        ((2, 512, DH), BF),
        ((2, 512, DH), BF),
        ((512, 512), F32),
        ((512, 512), BF),
        ((512, 512), BF),
        ((2, 2, 2, 512, DH), BF),
        ((2, 2, 2, 512, DH), BF),
        ((2, 4, 4, 2, 64, 512), F32),
        ((2, 2, 4, 4, 2, 16, 512), BF),
        ((2, 2, 4, 4, 2, 16, 512), BF),
        ((2, 2, 2, 4, 4, 16, 512), BF),
        ((2, 2, 3, 4, 16, 512), BF),
        ((2, 2, 3, 4, 16, 512), BF),
        ((2, 2, 4, 16, 512), BF),
        ((2, 2, 4, 16, 512), BF),
        ((2, 2, 3, 16, 512), BF),
        ((2, 2, 3, 16, 512), BF),
        ((2, 2, 2, 16, 512), BF),
        ((2, 2, 2, 16, 512), BF),
    ]
    qg, gk, gv, eg = pl.pallas_call(
        kernel,
        out_shape=[
            jax.ShapeDtypeStruct((512, 512), BF),
            jax.ShapeDtypeStruct((1024, 512), F32),
            jax.ShapeDtypeStruct((1024, 512), F32),
            jax.ShapeDtypeStruct((64, 512), F32),
        ],
        in_specs=[vm, vm, vm, hbm, hbm],
        out_specs=[hbm, hbm, hbm, vm],
        scratch_shapes=[pltpu.VMEM(*s) for s in scratch]
        + [
            pltpu.SemaphoreType.DMA((160,)),
            pltpu.SemaphoreType.DMA((160,)),
            pltpu.SemaphoreType.DMA((9,)),
        ],
        compiler_params=pltpu.CompilerParams(
            collective_id=0, has_side_effects=True, vmem_limit_bytes=60 * 1024 * 1024
        ),
        cost_estimate=pl.CostEstimate(
            flops=14_200_000_000, bytes_accessed=8_000_000, transcendentals=600_000
        ),
    )(encoder_out[0], queries[0, 0], ctx_grad[0, 0], key_weight[0], value_weight[0])
    qg, gk, gv, eg = hand_over(qg, gk, gv, eg)
    return qg[None, None], gk[None], gv[None], eg[None]


def solution(mesh):
    in_specs = (
        P("dp", "pipe", "tensor"),
        P("pipe", "dp", None, "tensor"),
        P("pipe", "dp", None, "tensor"),
        P("pipe", "dp", "tensor"),
        P("pipe", "dp", "tensor"),
    )
    out_specs = (
        P("pipe", "dp", None, "tensor"),
        P("pipe", "dp", "tensor"),
        P("pipe", "dp", "tensor"),
        P("dp", "pipe", "tensor"),
    )
    return jax.shard_map(shards, mesh=mesh, in_specs=in_specs, out_specs=out_specs, check_vma=False)
```

```python
import math

import jax
import jax.numpy as jnp
from jax import lax
from jax.experimental import pallas as pl
from jax.experimental.pallas import tpu as pltpu
from jax.sharding import PartitionSpec as P

DH = 256
BF = jnp.bfloat16
F32 = jnp.float32
MESH = pl.DeviceIdType.MESH
NT = (((1,), (1,)), ((), ()))
TN = (((0,), (0,)), ((), ()))


def mm(a, b):
    return jnp.dot(a, b, preferred_element_type=F32)


def kernel(
    enc, q, ctx, wk, wv,
    qg_out, gk_out, gv_out, eg,
    qg, gkv, encg, enc2, enct, wbuf, psk, psv, prk, prv, pown, krow, vrow, att, sl, al, kvg, kvg2,
    dacc, dsend, drecv, r1, ra_a, ra_b, r2a, r2b, rb_a, rb_b, fin, frecv,
    ssem, rsem, lsem,
):
    pi = lax.axis_index("pipe")
    ti = lax.axis_index("tensor")
    d = lax.axis_index("dp")
    y, c = pi // 2, pi % 2
    x, zh = ti // 2, ti % 2
    xh, xl = x // 2, x % 2
    dh, dl = d // 2, d % 2
    oc, oh, ol = 1 - c, 1 - dh, 1 - dl
    scale = 1.0 / math.sqrt(DH)
    mine = xl * 2 + xh
    lo, hi = pl.ds(0, 32), pl.ds(32, 32)

    def at(xx, zz, dd):
        return (pi, xx * 2 + zz, dd)

    def xpeer(k):
        return at((x + k) % 4, zh, d)

    def ypeer(k):
        return (((y + k) % 4) * 2 + c, ti, d)

    def xblock(k):
        xx = (x + k) % 4
        return (xx % 2) * 2 + xx // 2

    peer_c = (y * 2 + oc, ti, d)
    peer_l = at(x, zh, dh * 2 + ol)
    peer_h = at(x, zh, oh * 2 + dl)
    to_plane = [at(zh * 2 + xl, z, xh * 2 + dl) for z in range(2)]
    from_own = at(dh * 2 + xl, xh, dh * 2 + dl)
    from_oth = at(dh * 2 + xl, xh, oh * 2 + dl)
    loop = jnp.logical_and(xh == dh, zh == xh)
    more = dl != xl
    to_more = [at(dh * 2 + zh, z, xh * 2 + xl) for z in range(2)]
    from_more = at(dh * 2 + dl, xl, xh * 2 + ol)

    used = {"send": 0, "recv": 0}
    free = []

    def take(kind, n=1):
        used[kind] += n
        return used[kind] - n

    class Move:
        def __init__(self, src, dst, dev):
            self.k = free.pop() if free else take("send")
            self.copy = pltpu.make_async_remote_copy(
                src, dst, ssem.at[self.k], rsem.at[take("recv")], device_id=dev, device_id_type=MESH
            )

        def start(self):
            self.copy.start()

        def wait(self):
            self.copy.wait()
            free.append(self.k)

    send = Move

    def two_sems(src, dst, dev, ks, kr):
        return pltpu.make_async_remote_copy(
            src, dst, ssem.at[ks], rsem.at[kr], device_id=dev, device_id_type=MESH
        )

    barrier = pltpu.get_barrier_semaphore()

    def greet(dev):
        pl.semaphore_signal(barrier, inc=1, device_id=dev, device_id_type=MESH)

    peers = [peer_c, peer_l, peer_h]
    peers += [xpeer(k) for k in (1, 2, 3)] + [ypeer(k) for k in (1, 2, 3)]
    for dev in peers:
        greet(dev)
    greet(from_oth)
    greet(from_more)

    @pl.when(jnp.logical_not(loop))
    def _():
        greet(from_own)

    for z in range(2):

        @pl.when(jnp.logical_not(jnp.logical_and(loop, zh == z)))
        def _(z=z):
            greet(to_plane[z])

    owns = []
    for h in range(2):
        for kv, w in enumerate((wk, wv)):
            cp = pltpu.make_async_copy(
                w.at[:, pl.ds(h * DH, DH)], wbuf.at[h, kv, dl], lsem.at[h * 2 + kv]
            )
            cp.start()
            owns.append(cp)

    pl.semaphore_wait(
        barrier, len(peers) + jnp.where(loop, 2, 4) + jnp.where(more, 2, 0)
    )

    ks, kr = take("send", 2), take("recv", 2)
    piece = encg.at[dh, xl * 2 + zh, y, c]
    out_piece = [two_sems(enc, piece, to_plane[z], ks + z, kr + dh) for z in range(2)]
    for z in range(2):

        @pl.when(jnp.logical_not(jnp.logical_and(loop, zh == z)))
        def _(z=z):
            out_piece[z].start()

    @pl.when(loop)
    def _():
        encg[dh, mine, y, c] = enc[...]

    ks2, kr2 = take("send", 2), take("recv")
    extra = enc2.at[dh, zh, y, c]
    out_more = [two_sems(enc, extra, to_more[z], ks2 + z, kr2) for z in range(2)]

    wsend = [
        [send(w.at[:, pl.ds(h * DH, DH)], wbuf.at[h, kv, dl], peer_l) for kv, w in enumerate((wk, wv))]
        for h in range(2)
    ]
    wsend[0][0].start()

    def piece_in(s):
        return two_sems(enc, encg.at[s, mine, y, c], from_oth, ks, kr + s)

    def gather_one(s):
        cps = []
        for k in (1, 2, 3):
            ref = encg.at[s, mine, y, c, lo]
            cps.append(send(ref, ref, xpeer(k)))
            ref = encg.at[s, mine, y, c, hi]
            cps.append(send(ref, ref, ypeer(k)))
        for cp in cps:
            cp.start()
        return cps

    def gather_two(s):
        cps = []
        for k in (1, 2, 3):
            ref = encg.at[s, :, y, c, lo]
            cps.append(send(ref, ref, ypeer(k)))
            ref = encg.at[s, mine, :, c, hi]
            cps.append(send(ref, ref, xpeer(k)))
        for cp in cps:
            cp.start()
        return cps

    def gather_core(s):
        ref = encg.at[s, :, :, c]
        cp = send(ref, ref, peer_c)
        cp.start()
        return cp

    def wait_all(cps):
        for cp in cps:
            cp.wait()

    piece_in(oh).wait_recv()
    g1o = gather_one(oh)

    @pl.when(jnp.logical_not(loop))
    def _():
        piece_in(dh).wait_recv()

    @pl.when(more)
    def _():
        for z in range(2):
            out_more[z].start()

    g1d = gather_one(dh)
    for z in range(2):

        @pl.when(jnp.logical_not(jnp.logical_and(loop, zh == z)))
        def _(z=z):
            out_piece[z].wait_send()

    wait_all(g1o)
    g2o = gather_two(oh)
    wsend[0][1].start()
    wait_all(g1d)
    wait_all(g2o)
    g3o = gather_core(oh)
    g2d = gather_two(dh)

    def project_rows(s, h, kv, cc):
        blocks = [encg[s, fb, :, cc].reshape(256, 512) for fb in range(4)]
        v = mm(jnp.concatenate(blocks, axis=1), wbuf[h, kv].reshape(2048, DH))
        return v.reshape(4, 64, DH)

    part = {}

    def project_send(h, kv):
        owns[h * 2 + kv].wait()
        wsend[h][kv].wait()

        def step(cc, carry):
            v = project_rows(oh, h, kv, cc)
            if kv:
                psv[h, :, cc] = v.astype(BF)
            else:
                psk[h, :, cc] = v
            return carry

        lax.fori_loop(0, 2, step, 0)
        cp = send(psv.at[h], prv.at[h], peer_h) if kv else send(psk.at[h], prk.at[h], peer_h)
        cp.start()
        part[h, kv] = [cp]

    def project_own(h, kv):
        def step(cc, carry):
            pown[h, kv, :, cc] = project_rows(dh, h, kv, cc)
            return carry

        lax.fori_loop(0, 2, step, 0)

    owns[0].wait()
    wsend[0][0].wait()
    halves = []
    for cc in (c, oc):
        if len(halves) == 1:
            g3o.wait()
        psk[0, :, cc] = project_rows(oh, 0, 0, cc)
        ref = (psk.at[0, :, cc], prk.at[0, :, cc])
        halves.append(send(*ref, peer_h))
        halves[-1].start()
    part[0, 0] = halves
    wsend[1][0].start()
    project_send(0, 1)
    wsend[1][1].start()
    wait_all(g2d)
    g3d = gather_core(dh)

    @pl.when(more)
    def _():
        for z in range(2):
            out_more[z].wait_send()

    two_sems(enc, enc2.at[xh, xl, y, c], from_more, ks2, kr2).wait_recv()
    m1 = []
    for k in (1, 2, 3):
        ref = enc2.at[xh, xl, y, c]
        m1.append(send(ref, ref, xpeer(k)))
    for cp in m1:
        cp.start()
    g3d.wait()
    project_own(0, 0)
    project_own(0, 1)

    def flip(n, carry):
        s, z = n // 2, n % 2
        enct[s, z] = encg[s, dl * 2 + z].reshape(512, 512).T
        return carry

    lax.fori_loop(0, 4, flip, 0)
    project_send(1, 0)
    project_own(1, 0)
    project_send(1, 1)
    project_own(1, 1)
    wait_all(m1)
    m2 = []
    for k in (1, 2, 3):
        ref = enc2.at[:, :, y, c]
        m2.append(send(ref, ref, ypeer(k)))
    for cp in m2:
        cp.start()

    def flip2(n, carry):
        s, z = n // 2, n % 2
        enct[2 + s, z] = enc2[s, z].reshape(512, 512).T
        return carry

    grads = {}
    near = {}

    def grad_send(h, kv):
        ref = kvg.at[h, dh, kv]
        grads[h, kv] = send(ref, ref, peer_h)
        grads[h, kv].start()
        near[h, kv] = send(ref, kvg2.at[h, dh, kv], peer_l)
        near[h, kv].start()

    def attend(h):
        cols = pl.ds(h * DH, DH)
        wait_all(part[h, 0])
        krow[h] = (pown[h, 0] + prk[h]).reshape(512, DH).astype(BF)

        def soft(r, carry):
            rows = pl.ds(pl.multiple_of(r * 128, 128), 128)
            s = lax.dot_general(q[rows, cols], krow[h], NT, preferred_element_type=F32) * scale
            e = jnp.exp(s - jnp.max(s, axis=-1, keepdims=True))
            a = e / jnp.sum(e, axis=-1, keepdims=True)
            att[rows, :] = a
            al[rows, :] = a.astype(BF)
            return carry

        lax.fori_loop(0, 4, soft, 0)
        kvg[h, dh, 1] = lax.dot_general(
            al[...], ctx[:, cols], TN, preferred_element_type=F32
        ).astype(BF)
        grad_send(h, 1)
        wait_all(part[h, 1])
        vrow[h] = (pown[h, 1] + prv[h].astype(F32)).reshape(512, DH).astype(BF)

        def back(r, carry):
            rows = pl.ds(pl.multiple_of(r * 128, 128), 128)
            a = att[rows, :]
            p = lax.dot_general(ctx[rows, cols], vrow[h], NT, preferred_element_type=F32)
            g = a * (p - jnp.sum(p * a, axis=-1, keepdims=True))
            low = (g * scale).astype(BF)
            sl[rows, :] = low
            qg[rows, cols] = mm(low, krow[h]).astype(BF)
            return carry

        lax.fori_loop(0, 4, back, 0)
        kvg[h, dh, 0] = lax.dot_general(
            sl[...], q[:, cols], TN, preferred_element_type=F32
        ).astype(BF)
        grad_send(h, 0)

    attend(0)
    wait_all(m2)
    ref = enc2.at[:, :, :, c]
    m3 = send(ref, ref, peer_c)
    m3.start()
    attend(1)

    far = {}

    def forward(h, kv):
        grads[h, kv].wait()
        far[h, kv] = send(kvg.at[h, oh, kv], kvg2.at[h, oh, kv], peer_l)
        far[h, kv].start()

    def weight_rows(fb, terms):
        qt, half = fb // 2, pl.ds(pl.multiple_of((fb % 2) * 512, 512), 512)
        return jnp.concatenate([wbuf[h, kv, qt, half, :] for h, kv in terms], axis=1)

    def encoder_term(s, terms, add, out):
        def step(fb, carry):
            both = jnp.concatenate([kvg[h, s, kv] for h, kv in terms], axis=1)
            v = lax.dot_general(both, weight_rows(fb, terms), NT, preferred_element_type=F32)
            v = v.reshape(4, 2, 64, 512)
            dacc[s, fb] = dacc[s, fb] + v if add else v
            if out:
                for n in range(2):
                    for half in range(2):
                        rows = pl.ds(half * 32 + n * 16, 16)
                        dsend[s, n, fb, :, half] = dacc[s, fb, :, oc, rows, :].astype(BF)
            return carry

        lax.fori_loop(0, 4, step, 0)

    def reduce_core(s):
        cps = [send(dsend.at[s, n], drecv.at[s, n], peer_c) for n in range(2)]
        for cp in cps:
            cp.start()
        return cps

    def reduce_one(s, n, cp):
        cp.wait()
        for half in range(2):
            rows = pl.ds(half * 32 + n * 16, 16)

            def fold(fb, carry):
                v = dacc[s, fb, :, c, rows, :] + drecv[s, n, fb, :, half].astype(F32)
                r1[s, n, half, fb] = v.astype(BF)
                return carry

            lax.fori_loop(0, 4, fold, 0)
        cps = []
        for k in (1, 2, 3):
            cps.append(send(r1.at[s, n, 0, xblock(k)], ra_a.at[s, n, k - 1], xpeer(k)))
            cps.append(send(r1.at[s, n, 1, :, (y + k) % 4], ra_b.at[s, n, k - 1], ypeer(k)))
        for cp in cps:
            cp.start()
        return cps

    def reduce_two(s, n, cps):
        wait_all(cps)
        v = r1[s, n, 0, mine].astype(F32)
        w = r1[s, n, 1, :, y].astype(F32)
        for k in range(3):
            v = v + ra_a[s, n, k].astype(F32)
            w = w + ra_b[s, n, k].astype(F32)
        r2a[s, n] = v.astype(BF)
        r2b[s, n] = w.astype(BF)
        cps = []
        for k in (1, 2, 3):
            cps.append(send(r2a.at[s, n, (y + k) % 4], rb_a.at[s, n, k - 1], ypeer(k)))
            cps.append(send(r2b.at[s, n, xblock(k)], rb_b.at[s, n, k - 1], xpeer(k)))
        for cp in cps:
            cp.start()
        return cps

    def reduce_sum(s, n, cps):
        wait_all(cps)
        v = r2a[s, n, y].astype(F32)
        w = r2b[s, n, mine].astype(F32)
        for k in range(3):
            v = v + rb_a[s, n, k].astype(F32)
            w = w + rb_b[s, n, k].astype(F32)
        fin[s, n, 0] = v.astype(BF)
        fin[s, n, 1] = w.astype(BF)

    done = [pltpu.make_async_copy(qg, qg_out, lsem.at[8])]
    done[0].start()

    def weight_term(h, first):
        cols = pl.ds(h * DH, DH)

        def step(z, carry):
            rows = pl.ds(pl.multiple_of(z * 512, 512), 512)
            base, buf = (0, kvg) if first else (2, kvg2)
            lhs = jnp.concatenate([enct[base, z], enct[base + 1, z]], axis=1)
            rhs = jnp.concatenate(
                [jnp.concatenate([buf[h, s, 0], buf[h, s, 1]], axis=1) for s in range(2)], axis=0
            )
            v = mm(lhs, rhs)
            if first:
                gkv[h, 0, rows, :] = v[:, :DH]
                gkv[h, 1, rows, :] = v[:, DH:]
            else:
                gkv[h, 0, rows, :] += v[:, :DH]
                gkv[h, 1, rows, :] += v[:, DH:]
            return carry

        lax.fori_loop(0, 2, step, 0)
        if not first:
            for kv, out in enumerate((gk_out, gv_out)):
                done.append(pltpu.make_async_copy(gkv.at[h, kv], out.at[:, cols], lsem.at[4 + 2 * h + kv]))
                done[-1].start()

    every = [(0, 0), (0, 1), (1, 1), (1, 0)]
    encoder_term(dh, every, False, True)
    rc = reduce_core(dh)
    rs = [reduce_one(dh, n, rc[n]) for n in range(2)]
    m3.wait()
    lax.fori_loop(0, 4, flip2, 0)
    forward(0, 1)
    forward(0, 0)
    rs = [reduce_two(dh, n, rs[n]) for n in range(2)]
    weight_term(0, True)
    kf, krf = take("send", 4), take("recv", 4)

    out_own = [two_sems(fin.at[dh, n], frecv.at[zh, n], from_own, kf + n, krf + 2 * n + zh) for n in range(2)]
    out_oth = [two_sems(fin.at[oh, n], frecv.at[zh, n], from_oth, kf + 2 + n, krf + 2 * n + zh) for n in range(2)]

    forward(1, 1)
    encoder_term(oh, every[:3], False, False)
    forward(1, 0)
    encoder_term(oh, every[3:], True, True)
    rc = reduce_core(oh)
    for n in range(2):
        reduce_sum(dh, n, rs[n])

    @pl.when(jnp.logical_not(loop))
    def _():
        for cp in out_own:
            cp.start()

    @pl.when(loop)
    def _():
        frecv[zh] = fin[dh]

    rs = [reduce_one(oh, n, rc[n]) for n in range(2)]
    weight_term(1, True)
    rs[0] = reduce_two(oh, 0, rs[0])
    for kv in (1, 0):
        near[0, kv].wait()
        far[0, kv].wait()
    weight_term(0, False)
    rs[1] = reduce_two(oh, 1, rs[1])
    reduce_sum(oh, 0, rs[0])
    out_oth[0].start()
    reduce_sum(oh, 1, rs[1])
    out_oth[1].start()
    for kv in (1, 0):
        near[1, kv].wait()
        far[1, kv].wait()
    weight_term(1, False)

    @pl.when(jnp.logical_not(loop))
    def _():
        for cp in out_own:
            cp.wait_send()

    for cp in out_oth:
        cp.wait_send()
    for z in range(2):

        @pl.when(jnp.logical_not(jnp.logical_and(loop, zh == z)))
        def _(z=z):
            for n in range(2):
                two_sems(fin.at[0, n], frecv.at[z, n], to_plane[z], kf, krf + 2 * n + z).wait_recv()

    for n in range(2):
        for half in range(2):
            v = frecv[0, n, half].astype(F32) + frecv[1, n, half].astype(F32)
            eg[half * 32 + n * 16 : half * 32 + n * 16 + 16, :] = v
    for cp in done:
        cp.wait()


def hand_over(*arrays):
    n, steps = len(arrays), 2

    def kernel(*refs):
        for i in range(n):
            refs[n + i][...] = refs[i][...]

    specs = [pl.BlockSpec((a.shape[0] // steps, a.shape[1]), lambda i: (i, 0)) for a in arrays]
    return pl.pallas_call(
        kernel,
        grid=(steps,),
        out_shape=[jax.ShapeDtypeStruct(a.shape, a.dtype) for a in arrays],
        in_specs=specs,
        out_specs=specs,
    )(*arrays)


def shards(encoder_out, queries, ctx_grad, key_weight, value_weight):
    vm = pl.BlockSpec(memory_space=pltpu.VMEM)
    hbm = pl.BlockSpec(memory_space=pl.ANY)
    scratch = [
        ((512, 512), BF),
        ((2, 2, 1024, DH), F32),
        ((2, 4, 4, 2, 64, 512), BF),
        ((2, 2, 4, 2, 64, 512), BF),
        ((4, 2, 512, 512), BF),
        ((2, 2, 2, 1024, DH), BF),
        ((2, 4, 2, 64, DH), F32),
        ((2, 4, 2, 64, DH), BF),
        ((2, 4, 2, 64, DH), F32),
        ((2, 4, 2, 64, DH), BF),
        ((2, 2, 4, 2, 64, DH), F32),
        ((2, 512, DH), BF),
        ((2, 512, DH), BF),
        ((512, 512), F32),
        ((512, 512), BF),
        ((512, 512), BF),
        ((2, 2, 2, 512, DH), BF),
        ((2, 2, 2, 512, DH), BF),
        ((2, 4, 4, 2, 64, 512), F32),
        ((2, 2, 4, 4, 2, 16, 512), BF),
        ((2, 2, 4, 4, 2, 16, 512), BF),
        ((2, 2, 2, 4, 4, 16, 512), BF),
        ((2, 2, 3, 4, 16, 512), BF),
        ((2, 2, 3, 4, 16, 512), BF),
        ((2, 2, 4, 16, 512), BF),
        ((2, 2, 4, 16, 512), BF),
        ((2, 2, 3, 16, 512), BF),
        ((2, 2, 3, 16, 512), BF),
        ((2, 2, 2, 16, 512), BF),
        ((2, 2, 2, 16, 512), BF),
    ]
    qg, gk, gv, eg = pl.pallas_call(
        kernel,
        out_shape=[
            jax.ShapeDtypeStruct((512, 512), BF),
            jax.ShapeDtypeStruct((1024, 512), F32),
            jax.ShapeDtypeStruct((1024, 512), F32),
            jax.ShapeDtypeStruct((64, 512), F32),
        ],
        in_specs=[vm, vm, vm, hbm, hbm],
        out_specs=[hbm, hbm, hbm, vm],
        scratch_shapes=[pltpu.VMEM(*s) for s in scratch]
        + [
            pltpu.SemaphoreType.DMA((30,)),
            pltpu.SemaphoreType.DMA((113,)),
            pltpu.SemaphoreType.DMA((9,)),
        ],
        compiler_params=pltpu.CompilerParams(
            collective_id=0, has_side_effects=True, vmem_limit_bytes=60 * 1024 * 1024
        ),
        cost_estimate=pl.CostEstimate(
            flops=14_200_000_000, bytes_accessed=8_000_000, transcendentals=600_000
        ),
    )(encoder_out[0], queries[0, 0], ctx_grad[0, 0], key_weight[0], value_weight[0])
    qg, gk, gv, eg = hand_over(qg, gk, gv, eg)
    return qg[None, None], gk[None], gv[None], eg[None]


def solution(mesh):
    in_specs = (
        P("dp", "pipe", "tensor"),
        P("pipe", "dp", None, "tensor"),
        P("pipe", "dp", None, "tensor"),
        P("pipe", "dp", "tensor"),
        P("pipe", "dp", "tensor"),
    )
    out_specs = (
        P("pipe", "dp", None, "tensor"),
        P("pipe", "dp", "tensor"),
        P("pipe", "dp", "tensor"),
        P("dp", "pipe", "tensor"),
    )
    return jax.shard_map(shards, mesh=mesh, in_specs=in_specs, out_specs=out_specs, check_vma=False)
```

```python
import math

import jax
import jax.numpy as jnp
from jax import lax
from jax.experimental import pallas as pl
from jax.experimental.pallas import tpu as pltpu
from jax.sharding import PartitionSpec as P

DH = 256
BF = jnp.bfloat16
F32 = jnp.float32
MESH = pl.DeviceIdType.MESH
NT = (((1,), (1,)), ((), ()))
TN = (((0,), (0,)), ((), ()))


def mm(a, b):
    return jnp.dot(a, b, preferred_element_type=F32)


def kernel(
    enc, q_in, ctx_in, wk, wv,
    qg_out, gk_out, gv_out, eg,
    q, ctx, qg, gkv, encg, enc2, enct, wbuf, psk, psv, prk, prv, pown, krow, vrow, att, sl, al, kvg, kvg2,
    dacc, dsend, drecv, r1, ra_a, ra_b, r2a, r2b, rb_a, rb_b, fin, frecv,
    ssem, rsem, lsem,
):
    pi = lax.axis_index("pipe")
    ti = lax.axis_index("tensor")
    d = lax.axis_index("dp")
    y, c = pi // 2, pi % 2
    x, zh = ti // 2, ti % 2
    xh, xl = x // 2, x % 2
    dh, dl = d // 2, d % 2
    oc, oh, ol = 1 - c, 1 - dh, 1 - dl
    scale = 1.0 / math.sqrt(DH)
    mine = xl * 2 + xh
    lo, hi = pl.ds(0, 32), pl.ds(32, 32)

    def at(xx, zz, dd):
        return (pi, xx * 2 + zz, dd)

    def xpeer(k):
        return at((x + k) % 4, zh, d)

    def ypeer(k):
        return (((y + k) % 4) * 2 + c, ti, d)

    def xblock(k):
        xx = (x + k) % 4
        return (xx % 2) * 2 + xx // 2

    peer_c = (y * 2 + oc, ti, d)
    peer_l = at(x, zh, dh * 2 + ol)
    peer_h = at(x, zh, oh * 2 + dl)
    to_plane = [at(zh * 2 + xl, z, xh * 2 + dl) for z in range(2)]
    from_own = at(dh * 2 + xl, xh, dh * 2 + dl)
    from_oth = at(dh * 2 + xl, xh, oh * 2 + dl)
    loop = jnp.logical_and(xh == dh, zh == xh)
    more = dl != xl
    to_more = [at(dh * 2 + zh, z, xh * 2 + xl) for z in range(2)]
    from_more = at(dh * 2 + dl, xl, xh * 2 + ol)

    used = {"send": 0, "recv": 0}
    free = []

    def take(kind, n=1):
        used[kind] += n
        return used[kind] - n

    class Move:
        def __init__(self, src, dst, dev):
            self.k = free.pop() if free else take("send")
            self.copy = pltpu.make_async_remote_copy(
                src, dst, ssem.at[self.k], rsem.at[take("recv")], device_id=dev, device_id_type=MESH
            )

        def start(self):
            self.copy.start()

        def wait(self):
            self.copy.wait()
            free.append(self.k)

    send = Move

    def two_sems(src, dst, dev, ks, kr):
        return pltpu.make_async_remote_copy(
            src, dst, ssem.at[ks], rsem.at[kr], device_id=dev, device_id_type=MESH
        )

    barrier = pltpu.get_barrier_semaphore()

    def greet(dev):
        pl.semaphore_signal(barrier, inc=1, device_id=dev, device_id_type=MESH)

    peers = [peer_c, peer_l, peer_h]
    peers += [xpeer(k) for k in (1, 2, 3)] + [ypeer(k) for k in (1, 2, 3)]
    for dev in peers:
        greet(dev)
    greet(from_oth)
    greet(from_more)

    @pl.when(jnp.logical_not(loop))
    def _():
        greet(from_own)

    for z in range(2):

        @pl.when(jnp.logical_not(jnp.logical_and(loop, zh == z)))
        def _(z=z):
            greet(to_plane[z])

    owns = []
    for h in range(2):
        for kv, w in enumerate((wk, wv)):
            cp = pltpu.make_async_copy(
                w.at[:, pl.ds(h * DH, DH)], wbuf.at[h, kv, dl], lsem.at[h * 2 + kv]
            )
            cp.start()
            owns.append(cp)

    pl.semaphore_wait(
        barrier, len(peers) + jnp.where(loop, 2, 4) + jnp.where(more, 2, 0)
    )

    ks, kr = take("send", 2), take("recv", 2)
    piece = encg.at[dh, xl * 2 + zh, y, c]
    out_piece = [two_sems(enc, piece, to_plane[z], ks + z, kr + dh) for z in range(2)]
    for z in range(2):

        @pl.when(jnp.logical_not(jnp.logical_and(loop, zh == z)))
        def _(z=z):
            out_piece[z].start()

    stay = pltpu.make_async_copy(enc, encg.at[dh, mine, y, c], lsem.at[9])

    @pl.when(loop)
    def _():
        stay.start()

    inputs = [
        pltpu.make_async_copy(q_in, q, lsem.at[10]),
        pltpu.make_async_copy(ctx_in, ctx, lsem.at[11]),
    ]
    for cp in inputs:
        cp.start()

    ks2, kr2 = take("send", 2), take("recv")
    extra = enc2.at[dh, zh, y, c]
    out_more = [two_sems(enc, extra, to_more[z], ks2 + z, kr2) for z in range(2)]

    wsend = [
        [send(w.at[:, pl.ds(h * DH, DH)], wbuf.at[h, kv, dl], peer_l) for kv, w in enumerate((wk, wv))]
        for h in range(2)
    ]
    wsend[0][0].start()

    def piece_in(s):
        return two_sems(enc, encg.at[s, mine, y, c], from_oth, ks, kr + s)

    def gather_one(s):
        cps = []
        for k in (1, 2, 3):
            ref = encg.at[s, mine, y, c, lo]
            cps.append(send(ref, ref, xpeer(k)))
            ref = encg.at[s, mine, y, c, hi]
            cps.append(send(ref, ref, ypeer(k)))
        for cp in cps:
            cp.start()
        return cps

    def gather_two(s):
        cps = []
        for k in (1, 2, 3):
            ref = encg.at[s, :, y, c, lo]
            cps.append(send(ref, ref, ypeer(k)))
            ref = encg.at[s, mine, :, c, hi]
            cps.append(send(ref, ref, xpeer(k)))
        for cp in cps:
            cp.start()
        return cps

    def gather_core(s):
        ref = encg.at[s, :, :, c]
        cp = send(ref, ref, peer_c)
        cp.start()
        return cp

    def wait_all(cps):
        for cp in cps:
            cp.wait()

    piece_in(oh).wait_recv()
    g1o = gather_one(oh)

    @pl.when(jnp.logical_not(loop))
    def _():
        piece_in(dh).wait_recv()

    @pl.when(more)
    def _():
        for z in range(2):
            out_more[z].start()

    @pl.when(loop)
    def _():
        stay.wait()

    g1d = gather_one(dh)
    for z in range(2):

        @pl.when(jnp.logical_not(jnp.logical_and(loop, zh == z)))
        def _(z=z):
            out_piece[z].wait_send()

    wait_all(g1o)
    g2o = gather_two(oh)
    wsend[0][1].start()
    wait_all(g1d)
    wait_all(g2o)
    g3o = gather_core(oh)
    g2d = gather_two(dh)

    def project_rows(s, h, kv, cc):
        blocks = [encg[s, fb, :, cc].reshape(256, 512) for fb in range(4)]
        v = mm(jnp.concatenate(blocks, axis=1), wbuf[h, kv].reshape(2048, DH))
        return v.reshape(4, 64, DH)

    part = {}

    def project_send(h, kv):
        owns[h * 2 + kv].wait()
        wsend[h][kv].wait()

        def step(cc, carry):
            v = project_rows(oh, h, kv, cc)
            if kv:
                psv[h, :, cc] = v.astype(BF)
            else:
                psk[h, :, cc] = v
            return carry

        lax.fori_loop(0, 2, step, 0)
        cp = send(psv.at[h], prv.at[h], peer_h) if kv else send(psk.at[h], prk.at[h], peer_h)
        cp.start()
        part[h, kv] = [cp]

    def project_own(h, kv):
        def step(cc, carry):
            pown[h, kv, :, cc] = project_rows(dh, h, kv, cc)
            return carry

        lax.fori_loop(0, 2, step, 0)

    owns[0].wait()
    wsend[0][0].wait()
    halves = []
    for cc in (c, oc):
        if len(halves) == 1:
            g3o.wait()
        psk[0, :, cc] = project_rows(oh, 0, 0, cc)
        ref = (psk.at[0, :, cc], prk.at[0, :, cc])
        halves.append(send(*ref, peer_h))
        halves[-1].start()
    part[0, 0] = halves
    wsend[1][0].start()
    project_send(0, 1)
    wsend[1][1].start()
    wait_all(g2d)
    g3d = gather_core(dh)

    @pl.when(more)
    def _():
        for z in range(2):
            out_more[z].wait_send()

    two_sems(enc, enc2.at[xh, xl, y, c], from_more, ks2, kr2).wait_recv()
    m1 = []
    for k in (1, 2, 3):
        ref = enc2.at[xh, xl, y, c]
        m1.append(send(ref, ref, xpeer(k)))
    for cp in m1:
        cp.start()
    g3d.wait()
    project_own(0, 0)
    project_own(0, 1)

    def flip(n, carry):
        s, z = n // 2, n % 2
        enct[s, z] = encg[s, dl * 2 + z].reshape(512, 512).T
        return carry

    lax.fori_loop(0, 4, flip, 0)
    project_send(1, 0)
    project_own(1, 0)
    project_send(1, 1)
    project_own(1, 1)
    wait_all(m1)
    m2 = []
    for k in (1, 2, 3):
        ref = enc2.at[:, :, y, c]
        m2.append(send(ref, ref, ypeer(k)))
    for cp in m2:
        cp.start()

    def flip2(n, carry):
        s, z = n // 2, n % 2
        enct[2 + s, z] = enc2[s, z].reshape(512, 512).T
        return carry

    grads = {}
    near = {}

    def grad_send(h, kv):
        ref = kvg.at[h, dh, kv]
        grads[h, kv] = send(ref, ref, peer_h)
        grads[h, kv].start()
        near[h, kv] = send(ref, kvg2.at[h, dh, kv], peer_l)
        near[h, kv].start()

    def attend(h):
        cols = pl.ds(h * DH, DH)
        wait_all(part[h, 0])
        krow[h] = (pown[h, 0] + prk[h]).reshape(512, DH).astype(BF)

        def soft(r, carry):
            rows = pl.ds(pl.multiple_of(r * 128, 128), 128)
            s = lax.dot_general(q[rows, cols], krow[h], NT, preferred_element_type=F32) * scale
            e = jnp.exp(s - jnp.max(s, axis=-1, keepdims=True))
            a = e / jnp.sum(e, axis=-1, keepdims=True)
            att[rows, :] = a
            al[rows, :] = a.astype(BF)
            return carry

        lax.fori_loop(0, 4, soft, 0)
        kvg[h, dh, 1] = lax.dot_general(
            al[...], ctx[:, cols], TN, preferred_element_type=F32
        ).astype(BF)
        grad_send(h, 1)
        wait_all(part[h, 1])
        vrow[h] = (pown[h, 1] + prv[h].astype(F32)).reshape(512, DH).astype(BF)

        def back(r, carry):
            rows = pl.ds(pl.multiple_of(r * 128, 128), 128)
            a = att[rows, :]
            p = lax.dot_general(ctx[rows, cols], vrow[h], NT, preferred_element_type=F32)
            g = a * (p - jnp.sum(p * a, axis=-1, keepdims=True))
            low = (g * scale).astype(BF)
            sl[rows, :] = low
            qg[rows, cols] = mm(low, krow[h]).astype(BF)
            return carry

        lax.fori_loop(0, 4, back, 0)
        kvg[h, dh, 0] = lax.dot_general(
            sl[...], q[:, cols], TN, preferred_element_type=F32
        ).astype(BF)
        grad_send(h, 0)

    for cp in inputs:
        cp.wait()
    attend(0)
    wait_all(m2)
    ref = enc2.at[:, :, :, c]
    m3 = send(ref, ref, peer_c)
    m3.start()
    attend(1)

    far = {}

    def forward(h, kv):
        grads[h, kv].wait()
        far[h, kv] = send(kvg.at[h, oh, kv], kvg2.at[h, oh, kv], peer_l)
        far[h, kv].start()

    def weight_rows(fb, terms):
        qt, half = fb // 2, pl.ds(pl.multiple_of((fb % 2) * 512, 512), 512)
        return jnp.concatenate([wbuf[h, kv, qt, half, :] for h, kv in terms], axis=1)

    def encoder_term(s, terms, add, out):
        def step(fb, carry):
            both = jnp.concatenate([kvg[h, s, kv] for h, kv in terms], axis=1)
            v = lax.dot_general(both, weight_rows(fb, terms), NT, preferred_element_type=F32)
            v = v.reshape(4, 2, 64, 512)
            dacc[s, fb] = dacc[s, fb] + v if add else v
            if out:
                for n in range(2):
                    for half in range(2):
                        rows = pl.ds(half * 32 + n * 16, 16)
                        dsend[s, n, fb, :, half] = dacc[s, fb, :, oc, rows, :].astype(BF)
            return carry

        lax.fori_loop(0, 4, step, 0)

    def reduce_core(s):
        cps = [send(dsend.at[s, n], drecv.at[s, n], peer_c) for n in range(2)]
        for cp in cps:
            cp.start()
        return cps

    def reduce_one(s, n, cp):
        cp.wait()
        for half in range(2):
            rows = pl.ds(half * 32 + n * 16, 16)

            def fold(fb, carry):
                v = dacc[s, fb, :, c, rows, :] + drecv[s, n, fb, :, half].astype(F32)
                r1[s, n, half, fb] = v.astype(BF)
                return carry

            lax.fori_loop(0, 4, fold, 0)
        cps = []
        for k in (1, 2, 3):
            cps.append(send(r1.at[s, n, 0, xblock(k)], ra_a.at[s, n, k - 1], xpeer(k)))
            cps.append(send(r1.at[s, n, 1, :, (y + k) % 4], ra_b.at[s, n, k - 1], ypeer(k)))
        for cp in cps:
            cp.start()
        return cps

    def reduce_two(s, n, cps):
        wait_all(cps)
        v = r1[s, n, 0, mine].astype(F32)
        w = r1[s, n, 1, :, y].astype(F32)
        for k in range(3):
            v = v + ra_a[s, n, k].astype(F32)
            w = w + ra_b[s, n, k].astype(F32)
        r2a[s, n] = v.astype(BF)
        r2b[s, n] = w.astype(BF)
        cps = []
        for k in (1, 2, 3):
            cps.append(send(r2a.at[s, n, (y + k) % 4], rb_a.at[s, n, k - 1], ypeer(k)))
            cps.append(send(r2b.at[s, n, xblock(k)], rb_b.at[s, n, k - 1], xpeer(k)))
        for cp in cps:
            cp.start()
        return cps

    def reduce_sum(s, n, cps):
        wait_all(cps)
        v = r2a[s, n, y].astype(F32)
        w = r2b[s, n, mine].astype(F32)
        for k in range(3):
            v = v + rb_a[s, n, k].astype(F32)
            w = w + rb_b[s, n, k].astype(F32)
        fin[s, n, 0] = v.astype(BF)
        fin[s, n, 1] = w.astype(BF)

    done = [pltpu.make_async_copy(qg, qg_out, lsem.at[8])]
    done[0].start()

    def weight_term(h, first):
        cols = pl.ds(h * DH, DH)

        def step(z, carry):
            rows = pl.ds(pl.multiple_of(z * 512, 512), 512)
            base, buf = (0, kvg) if first else (2, kvg2)
            lhs = jnp.concatenate([enct[base, z], enct[base + 1, z]], axis=1)
            rhs = jnp.concatenate(
                [jnp.concatenate([buf[h, s, 0], buf[h, s, 1]], axis=1) for s in range(2)], axis=0
            )
            v = mm(lhs, rhs)
            if first:
                gkv[h, 0, rows, :] = v[:, :DH]
                gkv[h, 1, rows, :] = v[:, DH:]
            else:
                gkv[h, 0, rows, :] += v[:, :DH]
                gkv[h, 1, rows, :] += v[:, DH:]
            return carry

        lax.fori_loop(0, 2, step, 0)
        if not first:
            for kv, out in enumerate((gk_out, gv_out)):
                done.append(pltpu.make_async_copy(gkv.at[h, kv], out.at[:, cols], lsem.at[4 + 2 * h + kv]))
                done[-1].start()

    every = [(0, 0), (0, 1), (1, 1), (1, 0)]
    encoder_term(dh, every, False, True)
    rc = reduce_core(dh)
    rs = [reduce_one(dh, n, rc[n]) for n in range(2)]
    m3.wait()
    lax.fori_loop(0, 4, flip2, 0)
    forward(0, 1)
    forward(0, 0)
    kf, krf = take("send", 4), take("recv", 4)

    out_own = [two_sems(fin.at[dh, n], frecv.at[zh, n], from_own, kf + n, krf + 2 * n + zh) for n in range(2)]
    out_oth = [two_sems(fin.at[oh, n], frecv.at[zh, n], from_oth, kf + 2 + n, krf + 2 * n + zh) for n in range(2)]

    forward(1, 1)
    rs = [reduce_two(dh, n, rs[n]) for n in range(2)]
    encoder_term(oh, every[:3], False, False)
    forward(1, 0)
    encoder_term(oh, every[3:], True, True)
    rc = reduce_core(oh)
    for n in range(2):
        reduce_sum(dh, n, rs[n])

    @pl.when(jnp.logical_not(loop))
    def _():
        for cp in out_own:
            cp.start()

    @pl.when(loop)
    def _():
        frecv[zh] = fin[dh]

    rs = [reduce_one(oh, n, rc[n]) for n in range(2)]
    weight_term(0, True)
    weight_term(1, True)
    rs[0] = reduce_two(oh, 0, rs[0])
    for kv in (1, 0):
        near[0, kv].wait()
        far[0, kv].wait()
    weight_term(0, False)
    rs[1] = reduce_two(oh, 1, rs[1])
    reduce_sum(oh, 0, rs[0])
    out_oth[0].start()
    reduce_sum(oh, 1, rs[1])
    out_oth[1].start()
    for kv in (1, 0):
        near[1, kv].wait()
        far[1, kv].wait()
    weight_term(1, False)

    @pl.when(jnp.logical_not(loop))
    def _():
        for cp in out_own:
            cp.wait_send()

    for cp in out_oth:
        cp.wait_send()
    for z in range(2):

        @pl.when(jnp.logical_not(jnp.logical_and(loop, zh == z)))
        def _(z=z):
            for n in range(2):
                two_sems(fin.at[0, n], frecv.at[z, n], to_plane[z], kf, krf + 2 * n + z).wait_recv()

    for n in range(2):
        for half in range(2):
            v = frecv[0, n, half].astype(F32) + frecv[1, n, half].astype(F32)
            eg[half * 32 + n * 16 : half * 32 + n * 16 + 16, :] = v
    for cp in done:
        cp.wait()


def hand_over(*arrays):
    n, steps = len(arrays), 2

    def kernel(*refs):
        for i in range(n):
            refs[n + i][...] = refs[i][...]

    specs = [pl.BlockSpec((a.shape[0] // steps, a.shape[1]), lambda i: (i, 0)) for a in arrays]
    return pl.pallas_call(
        kernel,
        grid=(steps,),
        out_shape=[jax.ShapeDtypeStruct(a.shape, a.dtype) for a in arrays],
        in_specs=specs,
        out_specs=specs,
    )(*arrays)


def shards(encoder_out, queries, ctx_grad, key_weight, value_weight):
    vm = pl.BlockSpec(memory_space=pltpu.VMEM)
    hbm = pl.BlockSpec(memory_space=pl.ANY)
    scratch = [
        ((512, 512), BF),
        ((512, 512), BF),
        ((512, 512), BF),
        ((2, 2, 1024, DH), F32),
        ((2, 4, 4, 2, 64, 512), BF),
        ((2, 2, 4, 2, 64, 512), BF),
        ((4, 2, 512, 512), BF),
        ((2, 2, 2, 1024, DH), BF),
        ((2, 4, 2, 64, DH), F32),
        ((2, 4, 2, 64, DH), BF),
        ((2, 4, 2, 64, DH), F32),
        ((2, 4, 2, 64, DH), BF),
        ((2, 2, 4, 2, 64, DH), F32),
        ((2, 512, DH), BF),
        ((2, 512, DH), BF),
        ((512, 512), F32),
        ((512, 512), BF),
        ((512, 512), BF),
        ((2, 2, 2, 512, DH), BF),
        ((2, 2, 2, 512, DH), BF),
        ((2, 4, 4, 2, 64, 512), F32),
        ((2, 2, 4, 4, 2, 16, 512), BF),
        ((2, 2, 4, 4, 2, 16, 512), BF),
        ((2, 2, 2, 4, 4, 16, 512), BF),
        ((2, 2, 3, 4, 16, 512), BF),
        ((2, 2, 3, 4, 16, 512), BF),
        ((2, 2, 4, 16, 512), BF),
        ((2, 2, 4, 16, 512), BF),
        ((2, 2, 3, 16, 512), BF),
        ((2, 2, 3, 16, 512), BF),
        ((2, 2, 2, 16, 512), BF),
        ((2, 2, 2, 16, 512), BF),
    ]
    qg, gk, gv, eg = pl.pallas_call(
        kernel,
        out_shape=[
            jax.ShapeDtypeStruct((512, 512), BF),
            jax.ShapeDtypeStruct((1024, 512), F32),
            jax.ShapeDtypeStruct((1024, 512), F32),
            jax.ShapeDtypeStruct((64, 512), F32),
        ],
        in_specs=[hbm] * 5,
        out_specs=[hbm, hbm, hbm, vm],
        scratch_shapes=[pltpu.VMEM(*s) for s in scratch]
        + [
            pltpu.SemaphoreType.DMA((30,)),
            pltpu.SemaphoreType.DMA((113,)),
            pltpu.SemaphoreType.DMA((12,)),
        ],
        compiler_params=pltpu.CompilerParams(
            collective_id=0, has_side_effects=True, vmem_limit_bytes=60 * 1024 * 1024
        ),
        cost_estimate=pl.CostEstimate(
            flops=14_200_000_000, bytes_accessed=8_000_000, transcendentals=600_000
        ),
    )(encoder_out[0], queries[0, 0], ctx_grad[0, 0], key_weight[0], value_weight[0])
    qg, gk, gv, eg = hand_over(qg, gk, gv, eg)
    return qg[None, None], gk[None], gv[None], eg[None]


def solution(mesh):
    in_specs = (
        P("dp", "pipe", "tensor"),
        P("pipe", "dp", None, "tensor"),
        P("pipe", "dp", None, "tensor"),
        P("pipe", "dp", "tensor"),
        P("pipe", "dp", "tensor"),
    )
    out_specs = (
        P("pipe", "dp", None, "tensor"),
        P("pipe", "dp", "tensor"),
        P("pipe", "dp", "tensor"),
        P("dp", "pipe", "tensor"),
    )
    return jax.shard_map(shards, mesh=mesh, in_specs=in_specs, out_specs=out_specs, check_vma=False)
```
